256 devices in a mesh: dp: 32 (over y, x, core), head: 8 (over z).
Axes of the slice: x: 4, y: 4, z: 8, core: 2. Of those that a mesh axis runs over, the one named last changes fastest.
Arguments:
- query_states: bfloat16 [32, 1024, 4096], P('dp', 'head'), may hold values from -6 to 6
- key_states: bfloat16 [32, 1024, 1024], P('dp', 'head'), may hold values from -6 to 6
- value_columns: bfloat16 [32, 1024, 1024], P('dp', 'head'), may hold values from -6 to 6
- seg_ids: int32 [32, 1024], P('dp'), may hold values from 0 to 8, never falling along the last dimension, each value on 1 to 256 neighbouring positions
- out_grad: bfloat16 [32, 1024, 4096], P('dp', 'head'), may hold values from -6 to 6
- out_weight: bfloat16 [4096, 4096], P(None, 'head'), may hold values from -0.09375 to 0.09375
Outputs:
- query_gradient: bfloat16 [32, 1024, 4096], P('dp', 'head')
- key_gradient: bfloat16 [32, 1024, 1024], P('dp', 'head')
- value_gradient: bfloat16 [32, 1024, 1024], P('dp', 'head')
- weight_grad: float32 [4096, 4096], P('dp', 'head')
The draws below stay inside these ranges and needn't reach their ends.
Inputs may be any that keep to these rules, and one draw needn't show every extreme that they name: `seg_ids`: segment 0 of every pack is its shared prompt, at the pack's start; segments 1 to 8 are the completions that follow it.
All inputs are finite; a program needn't handle non-finite values.
Results may differ from the reference program's by a relative error of at most 0.034.
Values may be sent and summed in bfloat16 or wider, within the bound.
No kernel may reach another device: no remote copies, remote signals or barrier semaphores. Data moves between devices by JAX's collectives and lax.ppermute only.
A program may use at most 128 MiB of HBM per device.

```python
import math
import jax
import jax.numpy as jnp
import numpy as np
from jax import lax

D = 4096
QUERY_HEADS = 32
KEY_VALUE_HEADS = 8
HEAD_SIZE = 128
NSEG = 9
PACK_TOKENS = 1024
PACK_TOTAL = 32
MOST = 256
N_DP = 32


def draw_query_states(key, part):
    key = jax.random.fold_in(key, 11)
    base_offset = jnp.clip(jax.random.normal(key, (PACK_TOTAL, PACK_TOKENS, QUERY_HEADS, HEAD_SIZE), jnp.float32), -4.5, 4.5)
    return base_offset.reshape(PACK_TOTAL, PACK_TOKENS, QUERY_HEADS * HEAD_SIZE).astype(jnp.bfloat16)


def draw_key_states(key, part):
    key = jax.random.fold_in(key, 12)
    base_offset = jnp.clip(jax.random.normal(key, (PACK_TOTAL, PACK_TOKENS, KEY_VALUE_HEADS, HEAD_SIZE), jnp.float32), -4.5, 4.5)
    return base_offset.reshape(PACK_TOTAL, PACK_TOKENS, KEY_VALUE_HEADS * HEAD_SIZE).astype(jnp.bfloat16)


def strengthened(values, own_key, source, target, parts, factor):
    def block_of(dim):
        return (jnp.arange(values.shape[dim]) // (values.shape[dim] // parts)).reshape((-1,) + (1,) * (values.ndim - 1 - dim))

    first = jax.random.permutation(own_key, parts)[block_of(target)]
    second = (block_of(target) + parts // 2) % parts
    return jnp.where((block_of(source) == first) | (block_of(source) == second), factor * values, values)


def shard_levels(key, extent, cuts, least, high):
    factor_of, own = 1.0, jax.random.fold_in(key, 6)
    for dim, shards_of in cuts:
        draws = jnp.exp(jax.random.uniform(jax.random.fold_in(own, dim), (shards_of,), jnp.float32, least / len(cuts), high / len(cuts)))
        factor_of = factor_of * jnp.repeat(draws, extent[dim] // shards_of).reshape([-1 if axis == dim else 1 for axis in range(len(extent))])
    return factor_of


def profile(amount, total, reach, skew):
    loads = [(1 << 20) // math.isqrt(rank ** skew) + 1 for rank in range(2, amount + 1)]
    surplus, given = total - reach - (amount - 1), [1] * (amount - 1)
    while surplus > 0:
        free = [i for i in range(amount - 1) if given[i] < reach]
        whole, left = sum([loads[i] for i in free]), surplus
        for i in free:
            extra = min(reach - given[i], max(1, left * loads[i] // whole), surplus)
            given[i] = given[i] + extra
            surplus = surplus - extra
    return np.array([reach] + given)


def uneven_parts(rng, number_of, total, bound, slope):
    if number_of == 2:
        one = jax.random.randint(rng, (), max(1, total - bound), min(bound, total - 1) + 1)
        return jnp.stack([one, total - one])
    tallies = jnp.asarray(profile(number_of, total, bound, slope), jnp.int32)
    couples = (number_of - 1) // 2
    donor, receiver = tallies[1:1 + 2 * couples:2], tallies[2:2 + 2 * couples:2]
    room = jnp.minimum(donor - 1, bound - receiver)
    moved = jax.random.randint(jax.random.fold_in(rng, 1), (couples,), 0, 1 << 20) % (room + 1)
    tallies = tallies.at[1:1 + 2 * couples:2].set(donor - moved).at[2:2 + 2 * couples:2].set(receiver + moved)
    return tallies[jax.random.permutation(jax.random.fold_in(rng, 2), number_of)]


def noise(own_key, dims, spread, limit, cuts=(), held_as=jnp.bfloat16):
    values = spread * jax.random.normal(own_key, dims, jnp.float32)
    if cuts:
        values = values * shard_levels(own_key, dims, cuts, -0.22, 0.18)
    return jnp.clip(values, -limit, limit).astype(held_as)


def heavy_noise(own_key, shape, scale, reach, cuts, heavy, kind=jnp.bfloat16):
    entries = scale * jax.random.normal(own_key, shape, jnp.float32)
    if cuts:
        entries = entries * shard_levels(own_key, shape, cuts, -0.22, 0.18)
    return jnp.clip(strengthened(entries, jax.random.fold_in(own_key, 3), *heavy), -reach, reach).astype(kind)


def setup_inputs(seed: int = 0) -> dict:
    arg_keys = jax.random.split(jax.random.key(seed), 7)
    return {
        "query_states": draw_query_states(jax.random.fold_in(arg_keys[6], 71), 0),
        "key_states": draw_key_states(jax.random.fold_in(arg_keys[6], 71), 0),
        "value_columns": noise(arg_keys[2], (PACK_TOTAL, PACK_TOKENS, KEY_VALUE_HEADS * HEAD_SIZE), 1.0, 6.0, ((0, 32), (1, 8))),
        "seg_ids": jax.vmap(lambda own: jnp.searchsorted(jnp.cumsum(uneven_parts(own, NSEG, PACK_TOKENS, MOST, 1)), jnp.arange(PACK_TOKENS), side="right"))(jax.random.split(arg_keys[3], PACK_TOTAL)).reshape((PACK_TOTAL, PACK_TOKENS)).astype(jnp.int32),
        "out_grad": heavy_noise(arg_keys[4], (PACK_TOTAL, PACK_TOKENS, D), 1.0, 6.0, ((0, 32), (1, 8)), (0, 2, 32, 2.75)),
        "out_weight": noise(arg_keys[5], (D, QUERY_HEADS * HEAD_SIZE), (QUERY_HEADS * HEAD_SIZE) ** -0.5, 0.09375, ((1, 8),)),
    }


def to_low(array):
    return lax.optimization_barrier(array.astype(jnp.bfloat16))

def visible_mask(seg_row):
    pack_length = seg_row.shape[0]
    position = jnp.arange(pack_length, dtype=jnp.int32)
    causal = position[None, :] <= position[:, None]
    same_segment = (seg_row[None, :] == 0) | (seg_row[None, :] == seg_row[:, None])
    return causal & same_segment

def pack_grads(pack_queries, pack_keys, pack_values, seg_row, grad_pack, out_weight):
    pack_length = pack_queries.shape[0]
    query_groups = QUERY_HEADS // KEY_VALUE_HEADS
    factor = HEAD_SIZE ** (-0.5)
    query_four_axes = pack_queries.reshape(pack_length, KEY_VALUE_HEADS, query_groups, HEAD_SIZE).astype(jnp.float32)
    key_three_axes = pack_keys.reshape(pack_length, KEY_VALUE_HEADS, HEAD_SIZE).astype(jnp.float32)
    value_three_axes = pack_values.reshape(pack_length, KEY_VALUE_HEADS, HEAD_SIZE).astype(jnp.float32)
    visible = visible_mask(seg_row)
    scores = jnp.einsum('igrd,jgd->grij', query_four_axes, key_three_axes) * factor
    masked = jnp.where(visible, scores, -jnp.inf)
    row_max = lax.optimization_barrier(jnp.max(masked, axis=-1, keepdims=True))
    exp_terms = jnp.exp(masked - row_max)
    soft_probs = exp_terms / lax.optimization_barrier(jnp.sum(exp_terms, axis=-1, keepdims=True))
    probs_wide = to_low(soft_probs).astype(jnp.float32)
    attn_low = to_low(jnp.einsum('grij,jgd->igrd', probs_wide, value_three_axes))
    attn_flat = attn_low.reshape(pack_length, QUERY_HEADS * HEAD_SIZE)
    weight_product = jnp.dot(grad_pack.T, attn_flat, preferred_element_type=jnp.float32)
    output_direction = to_low(jnp.dot(grad_pack, out_weight, preferred_element_type=jnp.float32))
    output_direction_four = output_direction.reshape(pack_length, KEY_VALUE_HEADS, query_groups, HEAD_SIZE).astype(jnp.float32)
    dprobs = jnp.einsum('igrd,jgd->grij', output_direction_four, value_three_axes)
    row_delta = lax.optimization_barrier(jnp.sum(output_direction_four * attn_low.astype(jnp.float32), axis=-1))
    row_delta = jnp.transpose(row_delta, (1, 2, 0))[..., None]
    dscores = to_low(soft_probs * (dprobs - row_delta)).astype(jnp.float32)
    query_gradient = (jnp.einsum('grij,jgd->igrd', dscores, key_three_axes) * factor).astype(jnp.bfloat16)
    key_gradient = (jnp.einsum('grij,igrd->jgd', dscores, query_four_axes) * factor).astype(jnp.bfloat16)
    value_gradient = jnp.einsum('grij,igrd->jgd', probs_wide, output_direction_four).astype(jnp.bfloat16)
    return (query_gradient.reshape(pack_length, QUERY_HEADS * HEAD_SIZE), key_gradient.reshape(pack_length, KEY_VALUE_HEADS * HEAD_SIZE), value_gradient.reshape(pack_length, KEY_VALUE_HEADS * HEAD_SIZE), weight_product)

def reference(query_states, key_states, value_columns, seg_ids, out_grad, out_weight):

    def one_step(total, pieces):
        pack_queries, pack_keys, pack_values, seg_row, grad_pack = pieces
        query_gradient, key_gradient, value_gradient, weight_product = pack_grads(pack_queries, pack_keys, pack_values, seg_row, grad_pack, out_weight)
        return (total + weight_product, (query_gradient, key_gradient, value_gradient))
    start_total = jnp.zeros((D, QUERY_HEADS * HEAD_SIZE), jnp.float32)
    total, stacked = lax.scan(one_step, start_total, (query_states, key_states, value_columns, seg_ids, out_grad))
    weight_grad = total / math.sqrt(N_DP * PACK_TOKENS)
    return (stacked[0], stacked[1], stacked[2], weight_grad)
```

```python
import math

import jax
import jax.numpy as jnp
from jax import lax
from jax.experimental import pallas as pl
from jax.experimental.pallas import tpu as pltpu
from jax.sharding import PartitionSpec as P

QUERY_HEADS = 32
KEY_VALUE_HEADS = 8
HEAD = 128
GROUP = QUERY_HEADS // KEY_VALUE_HEADS
TOK = 128
RING = 8
PACK = TOK * RING
PART = TOK // 2
LOCAL = GROUP * HEAD
HALF = LOCAL // 2
PROMPT = 256
NEAR = 384
FACTOR = HEAD ** (-0.5)
MASKED = -1e30
BF = jnp.bfloat16
F32 = jnp.float32
SMEM = pl.BlockSpec(memory_space=pltpu.SMEM)
VMEM = pl.BlockSpec(memory_space=pltpu.VMEM)


def params():
    return pltpu.CompilerParams(vmem_limit_bytes=24 * 1024 * 1024)


def cost(flops, bytes_accessed):
    return pl.CostEstimate(flops=flops, bytes_accessed=bytes_accessed, transcendentals=0)


def shape(dims, dtype):
    return jax.ShapeDtypeStruct(dims, dtype)


def contract_rows(left, right):
    return lax.dot_general(left, right, (((0,), (0,)), ((), ())), preferred_element_type=F32)


def contract_columns(left, right):
    return lax.dot_general(left, right, (((1,), (1,)), ((), ())), preferred_element_type=F32)


def stacked_heads(block):
    return jnp.concatenate([block[:, h * HEAD : (h + 1) * HEAD] for h in range(GROUP)], axis=0)


def near_start(block):
    return pl.multiple_of(jnp.clip(block - 2, 2, 5) * TOK, TOK)


def window(ref, start, column):
    columns = slice(column, column + HEAD)
    return jnp.concatenate(
        [ref[0:PROMPT, columns], ref[pl.ds(start, NEAR), columns]], axis=0
    )


def window_bias(block, start, seg_col, seg_row):
    first = pl.multiple_of(block * TOK, TOK)
    seg_query = seg_col[pl.ds(first, TOK), :]
    row = first + lax.broadcasted_iota(jnp.int32, (TOK, PROMPT), 0)
    col = lax.broadcasted_iota(jnp.int32, (TOK, PROMPT), 1)
    seg_key = seg_row[:, 0:PROMPT]
    prompt_part = (col <= row) & ((seg_key == 0) | (seg_key == seg_query))
    row = first + lax.broadcasted_iota(jnp.int32, (TOK, NEAR), 0)
    col = start + lax.broadcasted_iota(jnp.int32, (TOK, NEAR), 1)
    near_part = (col <= row) & (seg_row[:, pl.ds(start, NEAR)] == seg_query)
    bias = jnp.concatenate(
        [jnp.where(prompt_part, 0.0, MASKED), jnp.where(near_part, 0.0, MASKED)], axis=1
    )
    return jnp.concatenate([bias] * GROUP, axis=0)


def pack_kernel(query_ref, key_ref, value_ref, out_ref, sems):
    copies = []
    for t in range(RING):
        begin = 0
        for n, (ref, width) in enumerate(((query_ref, LOCAL), (key_ref, HEAD), (value_ref, HEAD))):
            copies.append(
                pltpu.make_async_copy(
                    ref.at[:, t * width : (t + 1) * width],
                    out_ref.at[t, :, begin : begin + width],
                    sems.at[3 * t + n],
                )
            )
            begin += width
    for copy in copies:
        copy.start()
    for copy in copies:
        copy.wait()


def forward_kernel(seg_col, seg_row, pack_ref, attn_ref, turned_ref, stat_ref):
    def one_block(block, carry):
        start = near_start(block)
        first = pl.multiple_of(block * TOK, TOK)
        keys = window(pack_ref, start, LOCAL)
        values = window(pack_ref, start, LOCAL + HEAD)
        queries = stacked_heads(pack_ref[pl.ds(first, TOK), 0:LOCAL])
        scores = contract_columns(queries, keys) * FACTOR + window_bias(
            block, start, seg_col, seg_row
        )
        row_max = jnp.max(scores, axis=1, keepdims=True)
        terms = jnp.exp(scores - row_max)
        inverse = 1.0 / jnp.sum(terms, axis=1, keepdims=True)
        probs = (terms * inverse).astype(BF)
        attn = jnp.dot(probs, values, preferred_element_type=F32)
        for h in range(GROUP):
            rows = slice(h * TOK, (h + 1) * TOK)
            attn_ref[pl.ds(first, TOK), rows] = attn[rows].astype(BF)
            turned_ref[rows, pl.ds(first, TOK)] = attn[rows].T.astype(BF)
        stat_ref[pl.ds(first, TOK), :] = jnp.concatenate(
            [row_max[h * TOK : (h + 1) * TOK] for h in range(GROUP)]
            + [inverse[h * TOK : (h + 1) * TOK] for h in range(GROUP)],
            axis=1,
        )
        return carry

    lax.fori_loop(0, RING, one_block, 0)


def make_step_kernel(count, first, last):
    def step_kernel(*refs):
        id_ref, me_ref, seg_col, seg_row, pack_ref, attn_ref, stat_ref, weight_ref = refs[:8]
        refs = refs[8:]
        halves, refs = refs[: 2 * count], refs[2 * count :]
        if not first:
            total_in, refs = refs[0], refs[1:]
        if last:
            earlier, (send_ref, total, grad_ref) = refs[: RING - 1], refs[RING - 1 :]
        else:
            query_outs, (total, grad_ref) = refs[:count], refs[count:]
        for n, half in enumerate(halves):
            grad_ref[n * PART : (n + 1) * PART, :] = half[...]
        direction = jnp.dot(
            grad_ref[...], weight_ref[...], preferred_element_type=F32
        ).astype(BF)
        if first:
            total[...] = jnp.zeros_like(total)
        else:
            total[...] = total_in[...]
        for n in range(count):
            block = id_ref[n]
            start = near_start(block)
            rows = pl.ds(pl.multiple_of(block * TOK, TOK), TOK)
            keys = window(pack_ref, start, LOCAL)
            values = window(pack_ref, start, LOCAL + HEAD)
            queries = stacked_heads(pack_ref[rows, 0:LOCAL])
            out_dir = stacked_heads(direction[n * TOK : (n + 1) * TOK])
            attn = stacked_heads(attn_ref[rows, :])
            stat = stat_ref[rows, :]
            row_max = jnp.concatenate([stat[:, h : h + 1] for h in range(GROUP)], axis=0)
            inverse = jnp.concatenate(
                [stat[:, GROUP + h : GROUP + h + 1] for h in range(GROUP)], axis=0
            )
            scores = contract_columns(queries, keys) * FACTOR + window_bias(
                block, start, seg_col, seg_row
            )
            probs = jnp.exp(scores - row_max) * inverse
            delta = jnp.sum(out_dir.astype(F32) * attn.astype(F32), axis=1, keepdims=True)
            dprobs = contract_columns(out_dir, values)
            dscores = (probs * (dprobs - delta)).astype(BF)
            dquery = (jnp.dot(dscores, keys, preferred_element_type=F32) * FACTOR).astype(BF)
            for h in range(GROUP):
                columns = slice(h * HEAD, (h + 1) * HEAD)
                if last:
                    send_ref[rows, columns] = dquery[h * TOK : (h + 1) * TOK]
                else:
                    query_outs[n][:, columns] = dquery[h * TOK : (h + 1) * TOK]
            dkeys = contract_rows(dscores, queries)
            dvalues = contract_rows(probs.astype(BF), out_dir)
            near = pl.ds(start, NEAR)
            total[0:PROMPT, 0:HEAD] += dkeys[0:PROMPT]
            total[0:PROMPT, HEAD:] += dvalues[0:PROMPT]
            total[near, 0:HEAD] += dkeys[PROMPT:]
            total[near, HEAD:] += dvalues[PROMPT:]
        if last:
            send_ref[:, LOCAL : LOCAL + HEAD] = (total[:, 0:HEAD] * FACTOR).astype(BF)
            send_ref[:, LOCAL + HEAD :] = total[:, HEAD:].astype(BF)
            me = me_ref[0]
            for n, k in enumerate(k for k in range(RING) if k != 4):
                rows = pl.ds(pl.multiple_of(lax.rem(me + k, RING) * TOK, TOK), TOK)
                send_ref[rows, 0:LOCAL] = earlier[n][...]

    return step_kernel


def attention_step(ids, me_arg, segs, state, weight, halves, total):
    count, first = len(halves) // 2, total is None
    operands = [ids, me_arg, *segs, *state, weight, *halves]
    if not first:
        operands.append(total)
    return call(
        make_step_kernel(count, first, False),
        operands,
        2,
        [shape((TOK, LOCAL), BF)] * count + [shape((PACK, 2 * HEAD), F32)],
        [pltpu.VMEM((count * TOK, weight.shape[0]), BF)],
        flops=count * 1200000000,
        bytes_accessed=12000000,
    )


def last_step(ids, me_arg, segs, state, weight, halves, total, earlier):
    return call(
        make_step_kernel(1, False, True),
        [ids, me_arg, *segs, *state, weight, *halves, total, *earlier],
        2,
        [shape((PACK, LOCAL + 2 * HEAD), BF)],
        [pltpu.VMEM((PACK, 2 * HEAD), F32), pltpu.VMEM((TOK, weight.shape[0]), BF)],
        flops=1200000000,
        bytes_accessed=12000000,
    )[0]


def weight_kernel(scalar_ref, turned_ref, *refs):
    pieces, (other_ref, mine_ref, stage) = refs[: 2 * RING], refs[2 * RING :]
    me, core = scalar_ref[0], scalar_ref[1]
    for k in range(RING):
        first = lax.rem(me + k, RING) * TOK
        for part in range(2):
            rows = pl.ds(pl.multiple_of(first + part * PART, PART), PART)
            stage[rows, :] = pieces[2 * k + part][...]
    both = jnp.dot(turned_ref[...], stage[...], preferred_element_type=F32).astype(BF)
    for n in range(2):
        one = both[:, 2 * n * HEAD : (2 * n + 1) * HEAD]
        two = both[:, (2 * n + 1) * HEAD : (2 * n + 2) * HEAD]

        @pl.when(core == 0)
        def even():
            mine_ref[n] = one
            other_ref[n] = two

        @pl.when(core == 1)
        def odd():
            mine_ref[n] = two
            other_ref[n] = one


def weight_terms(scalars, turned, halves):
    tile = 512
    blocks = halves[0].shape[1] // tile
    part = pl.BlockSpec((2, LOCAL, HEAD), lambda i: (i, 0, 0))
    return pl.pallas_call(
        weight_kernel,
        grid=(blocks,),
        out_shape=[shape((2 * blocks, LOCAL, HEAD), BF)] * 2,
        in_specs=[SMEM, pl.BlockSpec((LOCAL, PACK), lambda i: (0, 0))]
        + [pl.BlockSpec((PART, tile), lambda i: (0, i))] * len(halves),
        out_specs=[part, part],
        scratch_shapes=[pltpu.VMEM((PACK, tile), BF)],
        compiler_params=params(),
        cost_estimate=cost(4400000000, 13 << 20),
    )(scalars, turned, *halves)


def combine_kernel(place_ref, mine_ref, arrived_ref, *outs):
    y, x = place_ref[0], place_ref[1]
    for ky in range(4):
        to_y = lax.rem(y + ky, 4)
        for kx in range(4):
            to_x = lax.rem(x + kx, 4)
            block = to_y * 4 + to_x
            both = mine_ref[block].astype(F32) + arrived_ref[block].astype(F32)
            outs[kx][to_y] = both[0:HALF].astype(BF)
            outs[4 + ky][to_x] = both[HALF:].astype(BF)


def middle_kernel(place_ref, *refs):
    from_x, from_y, to_y, to_x = refs[0:4], refs[4:8], refs[8:12], refs[12:16]
    y, x = place_ref[0], place_ref[1]
    for k in range(4):
        at_y, at_x = lax.rem(y + k, 4), lax.rem(x + k, 4)
        to_y[k][...] = sum(ref[at_y].astype(F32) for ref in from_x).astype(to_y[k].dtype)
        to_x[k][...] = sum(ref[at_x].astype(F32) for ref in from_y).astype(to_x[k].dtype)


def make_final_kernel(scale):
    def final_kernel(*refs):
        out_ref = refs[8]
        for n in range(2):
            total = sum(ref[...].astype(F32) for ref in refs[4 * n : 4 * n + 4])
            out_ref[:, n * HALF : (n + 1) * HALF] = total.T * scale

    return final_kernel


def gather_kernel(in_ref, query_ref, key_ref, value_ref):
    for k in range(RING):
        narrow = slice(k * HEAD, (k + 1) * HEAD)
        query_ref[:, k * LOCAL : (k + 1) * LOCAL] = in_ref[k, :, 0:LOCAL]
        key_ref[:, narrow] = in_ref[k, :, LOCAL : LOCAL + HEAD]
        value_ref[:, narrow] = in_ref[k, :, LOCAL + HEAD :]


def exchange(value):
    return lax.all_to_all(value, "head", split_axis=0, concat_axis=0, tiled=True)


def call(kernel, operands, scalars, outs, scratch=(), flops=0, bytes_accessed=0):
    return pl.pallas_call(
        kernel,
        out_shape=outs,
        in_specs=[SMEM] * scalars + [VMEM] * (len(operands) - scalars),
        out_specs=[VMEM] * len(outs),
        scratch_shapes=list(scratch),
        compiler_params=params(),
        cost_estimate=cost(flops, bytes_accessed),
    )(*operands)


def along_ring(value, shift):
    return lax.ppermute(value, "head", [(i, (i + shift) % RING) for i in range(RING)])


def along_dp(value, dy, dx, dcore):
    pairs = []
    for y in range(4):
        for x in range(4):
            for core in range(2):
                to = (((y + dy) % 4) * 4 + (x + dx) % 4) * 2 + (core + dcore) % 2
                pairs.append(((y * 4 + x) * 2 + core, to))
    return lax.ppermute(value, "dp", pairs)


def shards(query_states, key_states, value_columns, seg_ids, out_grad, out_weight):
    width = out_grad.shape[2]
    kv_width = KEY_VALUE_HEADS * HEAD
    me = lax.axis_index("head").astype(jnp.int32)
    dp = lax.axis_index("dp").astype(jnp.int32)
    me_arg, scalars = me[None], jnp.stack([me, dp % 2])
    place = jnp.stack([dp // 8, (dp // 2) % 4])
    segs = (seg_ids.reshape(PACK, 1), seg_ids)
    own = [out_grad[0, :PART], out_grad[0, PART:]]
    up, down = [[half] for half in own], [[half] for half in own]

    def ring_step(part, *before):
        moved = along_ring(up[part][-1], 1), along_ring(down[part][-1], -1)
        moved, before = lax.optimization_barrier((moved, before))
        up[part].append(moved[0])
        down[part].append(moved[1])
        return before

    for part in (0, 1):
        ring_step(part)
    packed = pl.pallas_call(
        pack_kernel,
        out_shape=shape((RING, TOK, LOCAL + 2 * HEAD), BF),
        in_specs=[pl.BlockSpec(memory_space=pl.ANY)] * 3,
        out_specs=pl.BlockSpec(memory_space=pl.ANY),
        scratch_shapes=[pltpu.SemaphoreType.DMA((3 * RING,))],
        compiler_params=params(),
        cost_estimate=cost(0, 3 << 20),
    )(query_states[0], key_states[0], value_columns[0])
    pack = exchange(packed).reshape(PACK, LOCAL + 2 * HEAD)

    (pack,) = ring_step(0, pack)
    attn, turned, stat = call(
        forward_kernel,
        [*segs, pack],
        0,
        [shape((PACK, LOCAL), BF), shape((LOCAL, PACK), BF), shape((PACK, 2 * GROUP), F32)],
        flops=1400000000,
        bytes_accessed=5 << 20,
    )
    state = (pack, attn, stat)
    query_pieces = [None] * RING

    def pair_step(s, total):
        ids = jnp.stack([(me + RING - s) % RING, (me + s) % RING])
        query_pieces[RING - s], query_pieces[s], total = attention_step(
            ids,
            me_arg,
            segs,
            state,
            out_weight,
            [up[0][s], up[1][s], down[0][s], down[1][s]],
            total,
        )
        return total

    query_pieces[0], total = attention_step(
        me_arg, me_arg, segs, state, out_weight, own, None
    )
    (total,) = ring_step(1, total)
    ring_step(0)
    total = pair_step(1, total)
    up_far, total = lax.optimization_barrier((up[0][3], total))
    up_far = along_ring(up_far, 1)
    ring_step(1)
    total = pair_step(2, total)
    down_far, total = lax.optimization_barrier((down[1][3], total))
    far = [up_far, along_ring(down_far, -1)]
    total = pair_step(3, total)
    far, total = lax.optimization_barrier((far, total))
    send = last_step(
        ((me + 4) % RING)[None],
        me_arg,
        segs,
        state,
        out_weight,
        far,
        total,
        [piece for piece in query_pieces if piece is not None],
    )
    turned, send = lax.optimization_barrier((turned, send))
    blocks = [own]
    for s in range(1, 4):
        blocks.append([down[0][s], down[1][s]])
    blocks.append(far)
    for s in range(3, 0, -1):
        blocks.append([up[0][s], up[1][s]])
    other, mine = weight_terms(scalars, turned, [half for block in blocks for half in block])
    from_core = along_dp(other, 0, 0, 1)
    send, mine = lax.optimization_barrier((send, mine))
    received = exchange(send.reshape(RING, TOK, LOCAL + 2 * HEAD))
    halves = call(
        combine_kernel,
        [place, mine, from_core],
        1,
        [shape((4, HALF, HEAD), BF)] * 8,
        bytes_accessed=6 << 20,
    )
    from_x = [halves[0]] + [along_dp(halves[k], 0, k, 0) for k in range(1, 4)]
    from_y = [halves[4]] + [along_dp(halves[4 + k], k, 0, 0) for k in range(1, 4)]
    middle = call(
        middle_kernel,
        [place, *from_x, *from_y],
        1,
        ([shape((HALF, HEAD), F32)] + [shape((HALF, HEAD), BF)] * 3) * 2,
        bytes_accessed=3 << 20,
    )
    first_half = [middle[0]] + [along_dp(middle[k], k, 0, 0) for k in range(1, 4)]
    second_half = [middle[4]] + [along_dp(middle[4 + k], 0, k, 0) for k in range(1, 4)]
    (weight_grad,) = call(
        make_final_kernel(1.0 / math.sqrt(lax.axis_size("dp") * PACK)),
        [*first_half, *second_half],
        0,
        [shape((HEAD, LOCAL), F32)],
        bytes_accessed=1 << 20,
    )
    query_gradient, key_gradient, value_gradient = call(
        gather_kernel,
        [received],
        0,
        [
            shape((TOK, width), BF),
            shape((TOK, kv_width), BF),
            shape((TOK, kv_width), BF),
        ],
        bytes_accessed=3 << 20,
    )
    return (query_gradient[None], key_gradient[None], value_gradient[None], weight_grad)


def solution(mesh):
    in_specs = (
        P("dp", "head", None),
        P("dp", "head", None),
        P("dp", "head", None),
        P("dp", None),
        P("dp", "head", None),
        P(None, "head"),
    )
    out_specs = (
        P("dp", "head", None),
        P("dp", "head", None),
        P("dp", "head", None),
        P("dp", "head"),
    )
    return jax.shard_map(shards, mesh=mesh, in_specs=in_specs, out_specs=out_specs, check_vma=False)
```

```python
import math

import jax
import jax.numpy as jnp
from jax import lax
from jax.experimental import pallas as pl
from jax.experimental.pallas import tpu as pltpu
from jax.sharding import PartitionSpec as P

QUERY_HEADS = 32
KEY_VALUE_HEADS = 8
HEAD = 128
GROUP = QUERY_HEADS // KEY_VALUE_HEADS
TOK = 128
RING = 8
PACK = TOK * RING
BLOCKS = 16
LOCAL = GROUP * HEAD
HALF = LOCAL // 2
PROMPT = 256
NEAR = 384
FACTOR = HEAD ** (-0.5)
MASKED = -1e30
BF = jnp.bfloat16
F32 = jnp.float32
SMEM = pl.BlockSpec(memory_space=pltpu.SMEM)
VMEM = pl.BlockSpec(memory_space=pltpu.VMEM)
HBM = pl.BlockSpec(memory_space=pltpu.HBM)


def params():
    return pltpu.CompilerParams(vmem_limit_bytes=32 * 1024 * 1024)


def cost(flops, bytes_accessed):
    return pl.CostEstimate(flops=flops, bytes_accessed=bytes_accessed, transcendentals=0)


def contract_rows(left, right):
    return lax.dot_general(left, right, (((0,), (0,)), ((), ())), preferred_element_type=F32)


def contract_columns(left, right):
    return lax.dot_general(left, right, (((1,), (1,)), ((), ())), preferred_element_type=F32)


def stacked_heads(block):
    return jnp.concatenate([block[:, h * HEAD : (h + 1) * HEAD] for h in range(GROUP)], axis=0)


def tile_rows(block):
    return pl.ds(pl.multiple_of(block * TOK, TOK), TOK)


def near_start(block):
    return pl.multiple_of(jnp.clip(block - 2, 2, 5) * TOK, TOK)


def window(ref, start):
    return jnp.concatenate([ref[0:PROMPT, :], ref[pl.ds(start, NEAR), :]], axis=0)


def window_bias(block, start, seg_row):
    first = pl.multiple_of(block * TOK, TOK)
    seg_query = seg_row[:, pl.ds(first, TOK)].astype(F32)
    seg_query = jnp.broadcast_to(seg_query, (TOK, TOK)).T[:, 0:1]
    row = first + lax.broadcasted_iota(jnp.int32, (TOK, PROMPT), 0)
    col = lax.broadcasted_iota(jnp.int32, (TOK, PROMPT), 1)
    seg_key = seg_row[:, 0:PROMPT].astype(F32)
    prompt_part = (col <= row) & ((seg_key == 0.0) | (seg_key == seg_query))
    row = first + lax.broadcasted_iota(jnp.int32, (TOK, NEAR), 0)
    col = start + lax.broadcasted_iota(jnp.int32, (TOK, NEAR), 1)
    near_part = (col <= row) & (seg_row[:, pl.ds(start, NEAR)].astype(F32) == seg_query)
    bias = jnp.concatenate(
        [jnp.where(prompt_part, 0.0, MASKED), jnp.where(near_part, 0.0, MASKED)], axis=1
    )
    return jnp.concatenate([bias] * GROUP, axis=0)


class Copies:
    def __init__(self, sems):
        self.sems, self.used = sems, 0

    def start(self, source, target):
        copy = pltpu.make_async_copy(source, target, self.sems.at[self.used])
        self.used += 1
        copy.start()
        return copy


def finish(*copies):
    for copy in copies:
        copy.wait()


def arrange_kernel(core_ref, *refs):
    in_hbms, (out_hbm, other_hbm, mine_hbm), refs = refs[:4], refs[4:7], refs[7:]
    held, sems = refs[:4], refs[4]
    copies, core, pending = Copies(sems), core_ref[0], []
    arriving = [copies.start(source, target) for source, target in zip(in_hbms, held)]
    begin = 0
    for copy, ref, width in zip(arriving[:3], held[:3], (LOCAL, HEAD, HEAD)):
        copy.wait()
        for t in range(RING):
            pending.append(
                copies.start(
                    ref.at[:, t * width : (t + 1) * width],
                    out_hbm.at[t, :, begin : begin + width],
                )
            )
        begin += width
    arriving[3].wait()
    for n in range(BLOCKS):
        for target, side in ((other_hbm, 1 - core), (mine_hbm, core)):
            source = pl.ds(pl.multiple_of((2 * n + side) * HEAD, HEAD), HEAD)
            pending.append(
                copies.start(held[3].at[:, source], target.at[:, n * HEAD : (n + 1) * HEAD])
            )
    finish(*pending)


def spread_kernel(in_hbm, query_hbm, key_hbm, value_hbm, held, sems):
    copies, pending = Copies(sems), []
    arriving = [copies.start(in_hbm.at[t], held.at[t]) for t in range(RING)]
    for t in range(RING):
        arriving[t].wait()
        begin = 0
        for ref, width in ((query_hbm, LOCAL), (key_hbm, HEAD), (value_hbm, HEAD)):
            pending.append(
                copies.start(
                    held.at[t, :, begin : begin + width],
                    ref.at[:, t * width : (t + 1) * width],
                )
            )
            begin += width
    finish(*pending)


def forward_kernel(me_ref, seg_row, pack_hbm, attn_hbm, turned_hbm, stat_hbm, *scratch):
    query_ref, key_ref, value_ref, attn_ref, turned_ref, stat_ref, sems = scratch
    copies, me = Copies(sems), me_ref[0]
    finish(
        copies.start(pack_hbm.at[:, 0:LOCAL], query_ref),
        copies.start(pack_hbm.at[:, LOCAL : LOCAL + HEAD], key_ref),
        copies.start(pack_hbm.at[:, LOCAL + HEAD :], value_ref),
    )

    def one_block(block, carry):
        start = near_start(block)
        rows_of = tile_rows(block)
        queries = stacked_heads(query_ref[rows_of, :])
        scores = contract_columns(queries, window(key_ref, start)) * FACTOR
        scores = scores + window_bias(block, start, seg_row)
        row_max = jnp.max(scores, axis=1, keepdims=True)
        terms = jnp.exp(scores - row_max)
        inverse = 1.0 / jnp.sum(terms, axis=1, keepdims=True)
        probs = (terms * inverse).astype(BF)
        attn = jnp.dot(probs, window(value_ref, start), preferred_element_type=F32)
        turned = tile_rows(lax.rem(block + RING - me, RING))
        for h in range(GROUP):
            rows = slice(h * TOK, (h + 1) * TOK)
            attn_ref[rows_of, rows] = attn[rows].astype(BF)
            turned_ref[rows, turned] = attn[rows].T.astype(BF)
        stat_ref[rows_of, :] = jnp.concatenate(
            [row_max[h * TOK : (h + 1) * TOK] for h in range(GROUP)]
            + [inverse[h * TOK : (h + 1) * TOK] for h in range(GROUP)],
            axis=1,
        )
        return carry

    lax.fori_loop(0, RING, one_block, 0, unroll=4)
    finish(
        copies.start(attn_ref, attn_hbm),
        copies.start(turned_ref, turned_hbm),
        copies.start(stat_ref, stat_hbm),
    )


def make_step_kernel(count, first, last):
    def step_kernel(*refs):
        id_ref, core_ref, seg_row, pack_hbm, attn_hbm, stat_hbm, weight_hbm = refs[:7]
        refs = refs[7:]
        pieces, refs = refs[: 2 * count], refs[2 * count :]
        if not first:
            totals, refs = refs[0], refs[1:]
        if last:
            earlier, send_hbm, refs = refs[: RING - 1], refs[RING - 1], refs[RING:]
        else:
            out_hbms, total_hbm, refs = refs[:count], refs[count], refs[count + 1 :]
        grad_ref, weight_ref, key_ref, value_ref, query_ref, attn_ref, stat_ref = refs[:7]
        total, result_ref, sems = refs[7:]
        copies, core = Copies(sems), core_ref[0]
        blocks = [id_ref[n] for n in range(count)]
        width = pieces[0].shape[1]
        need_scores, need_grads, need_attn, need_total, moved = [], [], [], [], []
        need_scores.append(copies.start(pack_hbm.at[:, LOCAL : LOCAL + HEAD], key_ref))
        for n, block in enumerate(blocks):
            rows = tile_rows(block)
            need_scores.append(copies.start(pack_hbm.at[rows, 0:LOCAL], query_ref.at[n]))
            need_scores.append(copies.start(stat_hbm.at[rows, :], stat_ref.at[n]))
        for part, side in enumerate((1 - core, core)):
            need_grads.append(copies.start(weight_hbm.at[:, side], weight_ref.at[part]))
            for n in range(count):
                need_grads.append(
                    copies.start(
                        pieces[2 * n + part],
                        grad_ref.at[
                            n * TOK : (n + 1) * TOK, part * width : (part + 1) * width
                        ],
                    )
                )
        need_attn.append(copies.start(pack_hbm.at[:, LOCAL + HEAD :], value_ref))
        for n, block in enumerate(blocks):
            need_attn.append(copies.start(attn_hbm.at[tile_rows(block), :], attn_ref.at[n]))
        if not first:
            need_total.append(copies.start(totals, total))
        if last:
            me = lax.rem(blocks[0] + 4, RING)
            for n, k in enumerate(k for k in range(RING) if k != 4):
                rows = tile_rows(lax.rem(me + k, RING))
                moved.append(copies.start(earlier[n], result_ref.at[rows, 0:LOCAL]))
        finish(*need_scores)
        all_probs = []
        for n, block in enumerate(blocks):
            start = near_start(block)
            stat = stat_ref[n]
            row_max = jnp.concatenate([stat[:, h : h + 1] for h in range(GROUP)], axis=0)
            inverse = jnp.concatenate(
                [stat[:, GROUP + h : GROUP + h + 1] for h in range(GROUP)], axis=0
            )
            queries = stacked_heads(query_ref[n])
            scores = contract_columns(queries, window(key_ref, start)) * FACTOR
            scores = scores + window_bias(block, start, seg_row)
            all_probs.append(jnp.exp(scores - row_max) * inverse)
        finish(*need_grads)
        direction = jnp.dot(
            grad_ref[...],
            weight_ref[...].reshape(2 * width, LOCAL),
            preferred_element_type=F32,
        ).astype(BF)
        finish(*need_attn)
        finish(*need_total)
        if first:
            total[...] = jnp.zeros_like(total)
        for n, block in enumerate(blocks):
            start = near_start(block)
            probs = all_probs[n]
            keys = window(key_ref, start)
            queries = stacked_heads(query_ref[n])
            out_dir = stacked_heads(direction[n * TOK : (n + 1) * TOK])
            attn = stacked_heads(attn_ref[n])
            delta = jnp.sum(out_dir.astype(F32) * attn.astype(F32), axis=1, keepdims=True)
            dprobs = contract_columns(out_dir, window(value_ref, start))
            dscores = (probs * (dprobs - delta)).astype(BF)
            dquery = (jnp.dot(dscores, keys, preferred_element_type=F32) * FACTOR).astype(BF)
            for h in range(GROUP):
                columns = slice(h * HEAD, (h + 1) * HEAD)
                if last:
                    result_ref[tile_rows(block), columns] = dquery[h * TOK : (h + 1) * TOK]
                else:
                    result_ref[n, :, columns] = dquery[h * TOK : (h + 1) * TOK]
            if not last:
                moved.append(copies.start(result_ref.at[n], out_hbms[n]))
            dkeys = contract_rows(dscores, queries)
            dvalues = contract_rows(probs.astype(BF), out_dir)
            near = pl.ds(start, NEAR)
            total[0:PROMPT, 0:HEAD] += dkeys[0:PROMPT]
            total[0:PROMPT, HEAD:] += dvalues[0:PROMPT]
            total[near, 0:HEAD] += dkeys[PROMPT:]
            total[near, HEAD:] += dvalues[PROMPT:]
        if last:
            result_ref[:, LOCAL : LOCAL + HEAD] = (total[:, 0:HEAD] * FACTOR).astype(BF)
            result_ref[:, LOCAL + HEAD :] = total[:, HEAD:].astype(BF)
            finish(*moved)
            finish(copies.start(result_ref, send_hbm))
        else:
            finish(copies.start(total, total_hbm), *moved)

    return step_kernel


def attention_step(ids, core_arg, seg_row, state, weight, pieces, total, earlier=None):
    count, first, last = len(pieces) // 2, total is None, earlier is not None
    width = pieces[0].shape[1]
    operands = [ids, core_arg, seg_row, *state, weight, *pieces]
    if not first:
        operands.append(total)
    if last:
        operands += earlier
        outs = [((PACK, LOCAL + 2 * HEAD), BF)]
    else:
        outs = [((TOK, LOCAL), BF)] * count + [((PACK, 2 * HEAD), F32)]
    scratch = [
        pltpu.VMEM((count * TOK, 2 * width), BF),
        pltpu.VMEM((2, BLOCKS, HEAD, LOCAL), BF),
        pltpu.VMEM((PACK, HEAD), BF),
        pltpu.VMEM((PACK, HEAD), BF),
        pltpu.VMEM((count, TOK, LOCAL), BF),
        pltpu.VMEM((count, TOK, LOCAL), BF),
        pltpu.VMEM((count, TOK, 2 * GROUP), F32),
        pltpu.VMEM((PACK, 2 * HEAD), F32),
        pltpu.VMEM((PACK, LOCAL + 2 * HEAD) if last else (count, TOK, LOCAL), BF),
        pltpu.SemaphoreType.DMA((32,)),
    ]
    return call(
        make_step_kernel(count, first, last),
        2,
        operands,
        outs,
        scratch,
        in_vmem=1,
        flops=count * 1200000000,
        bytes_accessed=12000000,
    )


def start_chunk(copies, pieces, stage, chunk, place):
    width = stage.shape[2]
    columns = pl.ds(pl.multiple_of(place * width, width), width)
    return [
        copies.start(pieces[k].at[:, columns], stage.at[chunk, k * TOK : (k + 1) * TOK, :])
        for k in range(RING)
    ]


def weight_other_kernel(turned_hbm, *refs):
    pieces, (out_hbm, turned_ref, stage, out_ref, sems) = refs[:RING], refs[RING:]
    copies, moved = Copies(sems), []
    turned = copies.start(turned_hbm, turned_ref)
    arriving = [start_chunk(copies, pieces, stage, c, c) for c in range(4)]
    turned.wait()
    for c in range(4):
        finish(*arriving[c])
        both = jnp.dot(turned_ref[...], stage[c], preferred_element_type=F32).astype(BF)
        for n in range(4):
            out_ref[4 * c + n] = both[:, n * HEAD : (n + 1) * HEAD]
        part = pl.ds(4 * c, 4)
        moved.append(copies.start(out_ref.at[part], out_hbm.at[part]))
    finish(*moved)


def weight_mine_kernel(place_ref, turned_hbm, arrived_hbm, *refs):
    pieces, refs = refs[:RING], refs[RING:]
    out_hbms, (turned_ref, stage, arrived_ref, half_x, half_y, sems) = refs[:8], refs[8:]
    copies, moved, arriving = Copies(sems), [], []
    y, x = place_ref[0], place_ref[1]
    turned = copies.start(turned_hbm, turned_ref)
    for ky in range(4):
        to_y = lax.rem(y + ky, 4)
        arriving.append(start_chunk(copies, pieces, stage, ky, to_y))
        arriving[ky].append(
            copies.start(arrived_hbm.at[pl.ds(to_y * 4, 4)], arrived_ref.at[ky])
        )
    turned.wait()
    for ky in range(4):
        to_y = lax.rem(y + ky, 4)
        finish(*arriving[ky])
        sums = jnp.dot(turned_ref[...], stage[ky], preferred_element_type=F32)
        for to_x in range(4):
            both = sums[:, to_x * HEAD : (to_x + 1) * HEAD]
            both = (both + arrived_ref[ky, to_x].astype(F32)).astype(BF)
            half_x[lax.rem(to_x + 4 - x, 4), to_y] = both[0:HALF]
            half_y[ky, to_x] = both[HALF:]
        moved.append(copies.start(half_y.at[ky], out_hbms[4 + ky]))
    for kx in range(4):
        moved.append(copies.start(half_x.at[kx], out_hbms[kx]))
    finish(*moved)


def make_middle_kernel(axis):
    def middle_kernel(place_ref, *refs):
        arrived, outs = refs[0:4], refs[4:8]
        for k in range(4):
            at = lax.rem(place_ref[axis] + k, 4)
            outs[k][...] = sum(ref[at].astype(F32) for ref in arrived).astype(outs[k].dtype)

    return middle_kernel


def make_final_kernel(scale):
    def final_kernel(*refs):
        out_ref = refs[8]
        for n in range(2):
            total = sum(ref[...].astype(F32) for ref in refs[4 * n : 4 * n + 4])
            out_ref[:, n * HALF : (n + 1) * HALF] = total.T * scale

    return final_kernel


def call(kernel, scalars, operands, outs, scratch=(), in_vmem=0, flops=0, bytes_accessed=0):
    split = scalars + in_vmem
    placed = [pltpu.with_memory_space_constraint(value, pltpu.HBM) for value in operands[split:]]
    return pl.pallas_call(
        kernel,
        out_shape=[pltpu.HBM(dims, dtype) for dims, dtype in outs],
        in_specs=[SMEM] * scalars + [VMEM] * in_vmem + [HBM] * len(placed),
        out_specs=[HBM] * len(outs),
        scratch_shapes=list(scratch),
        compiler_params=params(),
        cost_estimate=cost(flops, bytes_accessed),
    )(*operands[:split], *placed)


def call_vmem(kernel, scalars, operands, outs, bytes_accessed):
    return pl.pallas_call(
        kernel,
        out_shape=[jax.ShapeDtypeStruct(dims, dtype) for dims, dtype in outs],
        in_specs=[SMEM] * scalars + [VMEM] * (len(operands) - scalars),
        out_specs=[VMEM] * len(outs),
        compiler_params=params(),
        cost_estimate=cost(0, bytes_accessed),
    )(*operands)


def exchange(value):
    return lax.all_to_all(value, "head", split_axis=0, concat_axis=0, tiled=True)


def along_ring(value, shift):
    return lax.ppermute(value, "head", [(i, (i + shift) % RING) for i in range(RING)])


def along_dp(value, dy, dx, dcore):
    pairs = []
    for y in range(4):
        for x in range(4):
            for core in range(2):
                to = (((y + dy) % 4) * 4 + (x + dx) % 4) * 2 + (core + dcore) % 2
                pairs.append(((y * 4 + x) * 2 + core, to))
    return lax.ppermute(value, "dp", pairs)


def shards(query_states, key_states, value_columns, seg_ids, out_grad, out_weight):
    width = out_grad.shape[2]
    half = width // 2
    kv_width = KEY_VALUE_HEADS * HEAD
    joint = (RING, TOK, LOCAL + 2 * HEAD)
    me = lax.axis_index("head").astype(jnp.int32)
    dp = lax.axis_index("dp").astype(jnp.int32)
    me_arg, core_arg = me[None], (dp % 2)[None]
    place = jnp.stack([dp // 8, (dp // 2) % 4])
    weight = out_weight.reshape(BLOCKS, 2, HEAD, LOCAL)

    packed, other0, mine0 = call(
        arrange_kernel,
        1,
        [core_arg, query_states[0], key_states[0], value_columns[0], out_grad[0]],
        [(joint, BF), ((TOK, half), BF), ((TOK, half), BF)],
        [
            pltpu.VMEM((TOK, width), BF),
            pltpu.VMEM((TOK, kv_width), BF),
            pltpu.VMEM((TOK, kv_width), BF),
            pltpu.VMEM((TOK, width), BF),
            pltpu.SemaphoreType.DMA((4 + 3 * RING + 2 * BLOCKS,)),
        ],
        bytes_accessed=5 << 20,
    )
    up, down = [[other0], [mine0]], [[other0], [mine0]]

    def ring_step(part, *before):
        moved = along_ring(up[part][-1], 1), along_ring(down[part][-1], -1)
        moved, before = lax.optimization_barrier((moved, before))
        up[part].append(moved[0])
        down[part].append(moved[1])
        return before

    pack = exchange(packed).reshape(PACK, LOCAL + 2 * HEAD)
    (pack,) = ring_step(0, pack)
    attn, turned, stat = call(
        forward_kernel,
        1,
        [me_arg, seg_ids, pack],
        [((PACK, LOCAL), BF), ((LOCAL, PACK), BF), ((PACK, 2 * GROUP), F32)],
        [
            pltpu.VMEM((PACK, LOCAL), BF),
            pltpu.VMEM((PACK, HEAD), BF),
            pltpu.VMEM((PACK, HEAD), BF),
            pltpu.VMEM((PACK, LOCAL), BF),
            pltpu.VMEM((LOCAL, PACK), BF),
            pltpu.VMEM((PACK, 2 * GROUP), F32),
            pltpu.SemaphoreType.DMA((6,)),
        ],
        in_vmem=1,
        flops=1400000000,
        bytes_accessed=5 << 20,
    )
    (attn,) = ring_step(1, attn)
    ring_step(0)
    state = (pack, attn, stat)
    query_pieces = [None] * RING

    def both_ways(s):
        ids = [(me + RING - s) % RING, (me + s) % RING]
        return ids, [up[0][s], up[1][s], down[0][s], down[1][s]]

    def pair_step(s, total):
        ids, pieces = both_ways(s)
        query_pieces[RING - s], query_pieces[s], total = attention_step(
            jnp.stack(ids), core_arg, seg_ids, state, weight, pieces, total
        )
        return total

    ids, pieces = both_ways(1)
    query_pieces[0], query_pieces[7], query_pieces[1], total = attention_step(
        jnp.stack([me] + ids), core_arg, seg_ids, state, weight, [other0, mine0] + pieces, None
    )
    (total,) = ring_step(1, total)
    ring_step(0)
    total = pair_step(2, total)
    other_far = along_ring(up[0][3], 1)
    (total,) = ring_step(1, total)
    mine_far = along_ring(down[1][3], -1)
    total = pair_step(3, total)
    other_far, total = lax.optimization_barrier((other_far, total))

    def by_offset(part, far):
        return [up[part][0]] + down[part][1:4] + [far] + up[part][3:0:-1]

    stage = [pltpu.VMEM((LOCAL, PACK), BF), pltpu.VMEM((4, PACK, half // 4), BF)]
    (other,) = call(
        weight_other_kernel,
        0,
        [turned, *by_offset(0, other_far)],
        [((BLOCKS, LOCAL, HEAD), BF)],
        stage + [pltpu.VMEM((BLOCKS, LOCAL, HEAD), BF), pltpu.SemaphoreType.DMA((37,))],
        flops=2200000000,
        bytes_accessed=7 << 20,
    )
    from_core = along_dp(other, 0, 0, 1)
    mine_far, total, other = lax.optimization_barrier((mine_far, total, other))
    (send,) = attention_step(
        ((me + 4) % RING)[None],
        core_arg,
        seg_ids,
        state,
        weight,
        [other_far, mine_far],
        total,
        [piece for piece in query_pieces if piece is not None],
    )
    turned, send = lax.optimization_barrier((turned, send))
    halves = call(
        weight_mine_kernel,
        1,
        [place, turned, from_core, *by_offset(1, mine_far)],
        [((4, HALF, HEAD), BF)] * 8,
        stage
        + [pltpu.VMEM((4, 4, LOCAL, HEAD), BF)]
        + [pltpu.VMEM((4, 4, HALF, HEAD), BF)] * 2
        + [pltpu.SemaphoreType.DMA((45,))],
        flops=2200000000,
        bytes_accessed=9 << 20,
    )
    received = exchange(send.reshape(joint))
    shares = []
    for axis in range(2):
        own_half = halves[4 * axis : 4 * axis + 4]
        steps = [(0, k, 0) if axis == 0 else (k, 0, 0) for k in range(4)]
        arrived = [own_half[0]] + [along_dp(own_half[k], *steps[k]) for k in range(1, 4)]
        middle = call_vmem(
            make_middle_kernel(axis),
            1,
            [place, *arrived],
            [((HALF, HEAD), F32)] + [((HALF, HEAD), BF)] * 3,
            2 << 20,
        )
        steps = [(k, 0, 0) if axis == 0 else (0, k, 0) for k in range(4)]
        shares += [middle[0]] + [along_dp(middle[k], *steps[k]) for k in range(1, 4)]
    query_gradient, key_gradient, value_gradient = call(
        spread_kernel,
        0,
        [received],
        [((TOK, width), BF), ((TOK, kv_width), BF), ((TOK, kv_width), BF)],
        [pltpu.VMEM(joint, BF), pltpu.SemaphoreType.DMA((4 * RING,))],
        bytes_accessed=3 << 20,
    )
    shares[7], query_gradient = lax.optimization_barrier((shares[7], query_gradient))
    weight_grad = pl.pallas_call(
        make_final_kernel(1.0 / math.sqrt(lax.axis_size("dp") * PACK)),
        out_shape=jax.ShapeDtypeStruct((HEAD, LOCAL), F32),
        compiler_params=params(),
        cost_estimate=cost(0, 1 << 20),
    )(*shares)
    return (query_gradient[None], key_gradient[None], value_gradient[None], weight_grad)


def solution(mesh):
    in_specs = (
        P("dp", "head", None),
        P("dp", "head", None),
        P("dp", "head", None),
        P("dp", None),
        P("dp", "head", None),
        P(None, "head"),
    )
    out_specs = (
        P("dp", "head", None),
        P("dp", "head", None),
        P("dp", "head", None),
        P("dp", "head"),
    )
    return jax.shard_map(shards, mesh=mesh, in_specs=in_specs, out_specs=out_specs, check_vma=False)
```

```python
import math

import jax
import jax.numpy as jnp
from jax import lax
from jax.experimental import pallas as pl
from jax.experimental.pallas import tpu as pltpu
from jax.sharding import PartitionSpec as P

QUERY_HEADS = 32
KEY_VALUE_HEADS = 8
HEAD = 128
GROUP = QUERY_HEADS // KEY_VALUE_HEADS
TOK = 128
RING = 8
PACK = TOK * RING
BLOCKS = 16
LOCAL = GROUP * HEAD
HALF = LOCAL // 2
PROMPT = 256
NEAR = 384
FACTOR = HEAD ** (-0.5)
MASKED = -1e30
BF = jnp.bfloat16
F32 = jnp.float32
SMEM = pl.BlockSpec(memory_space=pltpu.SMEM)
VMEM = pl.BlockSpec(memory_space=pltpu.VMEM)
HBM = pl.BlockSpec(memory_space=pltpu.HBM)


def params():
    return pltpu.CompilerParams(vmem_limit_bytes=32 * 1024 * 1024)


def cost(flops, bytes_accessed):
    return pl.CostEstimate(flops=flops, bytes_accessed=bytes_accessed, transcendentals=0)


def contract_rows(left, right):
    return lax.dot_general(left, right, (((0,), (0,)), ((), ())), preferred_element_type=F32)


def contract_columns(left, right):
    return lax.dot_general(left, right, (((1,), (1,)), ((), ())), preferred_element_type=F32)


def stacked_heads(block):
    return jnp.concatenate([block[:, h * HEAD : (h + 1) * HEAD] for h in range(GROUP)], axis=0)


def tile_rows(block):
    return pl.ds(pl.multiple_of(block * TOK, TOK), TOK)


def near_start(block):
    return pl.multiple_of(jnp.clip(block - 2, 2, 5) * TOK, TOK)


def window(ref, start):
    return jnp.concatenate([ref[0:PROMPT, :], ref[pl.ds(start, NEAR), :]], axis=0)


def window_bias(block, start, seg_row):
    first = pl.multiple_of(block * TOK, TOK)
    seg_query = seg_row[:, pl.ds(first, TOK)].astype(F32)
    seg_query = jnp.broadcast_to(seg_query, (TOK, TOK)).T[:, 0:1]
    row = first + lax.broadcasted_iota(jnp.int32, (TOK, PROMPT), 0)
    col = lax.broadcasted_iota(jnp.int32, (TOK, PROMPT), 1)
    seg_key = seg_row[:, 0:PROMPT].astype(F32)
    prompt_part = (col <= row) & ((seg_key == 0.0) | (seg_key == seg_query))
    row = first + lax.broadcasted_iota(jnp.int32, (TOK, NEAR), 0)
    col = start + lax.broadcasted_iota(jnp.int32, (TOK, NEAR), 1)
    near_part = (col <= row) & (seg_row[:, pl.ds(start, NEAR)].astype(F32) == seg_query)
    bias = jnp.concatenate(
        [jnp.where(prompt_part, 0.0, MASKED), jnp.where(near_part, 0.0, MASKED)], axis=1
    )
    return jnp.concatenate([bias] * GROUP, axis=0)


class Copies:
    def __init__(self, sems):
        self.sems, self.used = sems, 0

    def start(self, source, target):
        copy = pltpu.make_async_copy(source, target, self.sems.at[self.used])
        self.used += 1
        copy.start()
        return copy


def finish(*copies):
    for copy in copies:
        copy.wait()


def pack_kernel(query_hbm, key_hbm, value_hbm, out_hbm, query_ref, key_ref, value_ref, sems):
    copies, pending, begin = Copies(sems), [], 0
    held = (query_ref, key_ref, value_ref)
    arriving = [copies.start(*pair) for pair in zip((query_hbm, key_hbm, value_hbm), held)]
    for copy, ref, width in zip(arriving, held, (LOCAL, HEAD, HEAD)):
        copy.wait()
        for t in range(RING):
            pending.append(
                copies.start(
                    ref.at[:, t * width : (t + 1) * width],
                    out_hbm.at[t, :, begin : begin + width],
                )
            )
        begin += width
    finish(*pending)


def split_kernel(core_ref, grad_hbm, other_hbm, mine_hbm, held, sems):
    copies, core, pending = Copies(sems), core_ref[0], []
    copies.start(grad_hbm, held).wait()
    for n in range(BLOCKS):
        for target, side in ((other_hbm, 1 - core), (mine_hbm, core)):
            source = pl.ds(pl.multiple_of((2 * n + side) * HEAD, HEAD), HEAD)
            pending.append(
                copies.start(held.at[:, source], target.at[:, n * HEAD : (n + 1) * HEAD])
            )
    finish(*pending)


def spread_kernel(in_ref, query_hbm, key_hbm, value_hbm, sems):
    copies, pending = Copies(sems), []
    for t in range(RING):
        begin = 0
        for target, width in ((query_hbm, LOCAL), (key_hbm, HEAD), (value_hbm, HEAD)):
            pending.append(
                copies.start(
                    in_ref.at[t, :, begin : begin + width],
                    target.at[:, t * width : (t + 1) * width],
                )
            )
            begin += width
    finish(*pending)


def forward_kernel(me_ref, seg_row, pack_hbm, attn_hbm, turned_hbm, stat_hbm, *scratch):
    query_ref, key_ref, value_ref, attn_ref, turned_ref, stat_ref, sems = scratch
    copies, me = Copies(sems), me_ref[0]
    finish(
        copies.start(pack_hbm.at[:, 0:LOCAL], query_ref),
        copies.start(pack_hbm.at[:, LOCAL : LOCAL + HEAD], key_ref),
        copies.start(pack_hbm.at[:, LOCAL + HEAD :], value_ref),
    )

    def one_block(block, carry):
        start = near_start(block)
        rows_of = tile_rows(block)
        queries = stacked_heads(query_ref[rows_of, :])
        scores = contract_columns(queries, window(key_ref, start)) * FACTOR
        scores = scores + window_bias(block, start, seg_row)
        row_max = jnp.max(scores, axis=1, keepdims=True)
        terms = jnp.exp(scores - row_max)
        inverse = 1.0 / jnp.sum(terms, axis=1, keepdims=True)
        probs = (terms * inverse).astype(BF)
        attn = jnp.dot(probs, window(value_ref, start), preferred_element_type=F32)
        turned = tile_rows(lax.rem(block + RING - me, RING))
        for h in range(GROUP):
            rows = slice(h * TOK, (h + 1) * TOK)
            attn_ref[rows_of, rows] = attn[rows].astype(BF)
            turned_ref[rows, turned] = attn[rows].T.astype(BF)
        stat_ref[rows_of, :] = jnp.concatenate(
            [row_max[h * TOK : (h + 1) * TOK] for h in range(GROUP)]
            + [inverse[h * TOK : (h + 1) * TOK] for h in range(GROUP)],
            axis=1,
        )
        return carry

    lax.fori_loop(0, RING, one_block, 0, unroll=4)
    finish(
        copies.start(attn_ref, attn_hbm),
        copies.start(turned_ref, turned_hbm),
        copies.start(stat_ref, stat_hbm),
    )


def make_step_kernel(count, first, last):
    def step_kernel(*refs):
        id_ref, core_ref, seg_row, pack_hbm, attn_hbm, stat_hbm, weight_hbm = refs[:7]
        refs = refs[7:]
        pieces, refs = refs[: 2 * count], refs[2 * count :]
        if not first:
            totals, refs = refs[0], refs[1:]
        if last:
            earlier, send_hbm, refs = refs[: RING - 1], refs[RING - 1], refs[RING:]
        else:
            out_hbms, total_hbm, refs = refs[:count], refs[count], refs[count + 1 :]
        grad_ref, weight_ref, key_ref, value_ref, query_ref, attn_ref, stat_ref = refs[:7]
        total, result_ref, sems = refs[7:]
        copies, core = Copies(sems), core_ref[0]
        blocks = [id_ref[n] for n in range(count)]
        width = pieces[0].shape[1]
        need_scores, need_grads, need_attn, need_total, moved = [], ([], []), [], [], []
        need_scores.append(copies.start(pack_hbm.at[:, LOCAL : LOCAL + HEAD], key_ref))
        for n, block in enumerate(blocks):
            rows = tile_rows(block)
            need_scores.append(copies.start(pack_hbm.at[rows, 0:LOCAL], query_ref.at[n]))
            need_scores.append(copies.start(stat_hbm.at[rows, :], stat_ref.at[n]))
        for part, side in enumerate((1 - core, core)):
            need_grads[part].append(copies.start(weight_hbm.at[:, side], weight_ref.at[part]))
            for n in range(count):
                need_grads[part].append(
                    copies.start(
                        pieces[2 * n + part],
                        grad_ref.at[
                            n * TOK : (n + 1) * TOK, part * width : (part + 1) * width
                        ],
                    )
                )
        need_attn.append(copies.start(pack_hbm.at[:, LOCAL + HEAD :], value_ref))
        for n, block in enumerate(blocks):
            need_attn.append(copies.start(attn_hbm.at[tile_rows(block), :], attn_ref.at[n]))
        if not first:
            need_total.append(copies.start(totals, total))
        if last:
            me = lax.rem(blocks[0] + 4, RING)
            for n, k in enumerate(k for k in range(RING) if k != 4):
                rows = tile_rows(lax.rem(me + k, RING))
                moved.append(copies.start(earlier[n], result_ref.at[rows, 0:LOCAL]))
        finish(*need_scores)
        all_probs = []
        for n, block in enumerate(blocks):
            start = near_start(block)
            stat = stat_ref[n]
            row_max = jnp.concatenate([stat[:, h : h + 1] for h in range(GROUP)], axis=0)
            inverse = jnp.concatenate(
                [stat[:, GROUP + h : GROUP + h + 1] for h in range(GROUP)], axis=0
            )
            queries = stacked_heads(query_ref[n])
            scores = contract_columns(queries, window(key_ref, start)) * FACTOR
            scores = scores + window_bias(block, start, seg_row)
            all_probs.append(jnp.exp(scores - row_max) * inverse)
        direction = 0.0
        for part in range(2):
            finish(*need_grads[part])
            direction = direction + jnp.dot(
                grad_ref[:, part * width : (part + 1) * width],
                weight_ref[part].reshape(width, LOCAL),
                preferred_element_type=F32,
            )
        direction = direction.astype(BF)
        finish(*need_attn)
        finish(*need_total)
        if first:
            total[...] = jnp.zeros_like(total)
        for n, block in enumerate(blocks):
            start = near_start(block)
            probs = all_probs[n]
            keys = window(key_ref, start)
            queries = stacked_heads(query_ref[n])
            out_dir = stacked_heads(direction[n * TOK : (n + 1) * TOK])
            attn = stacked_heads(attn_ref[n])
            delta = jnp.sum(out_dir.astype(F32) * attn.astype(F32), axis=1, keepdims=True)
            dprobs = contract_columns(out_dir, window(value_ref, start))
            dscores = (probs * (dprobs - delta)).astype(BF)
            dquery = (jnp.dot(dscores, keys, preferred_element_type=F32) * FACTOR).astype(BF)
            for h in range(GROUP):
                columns = slice(h * HEAD, (h + 1) * HEAD)
                if last:
                    result_ref[tile_rows(block), columns] = dquery[h * TOK : (h + 1) * TOK]
                else:
                    result_ref[n, :, columns] = dquery[h * TOK : (h + 1) * TOK]
            if not last:
                moved.append(copies.start(result_ref.at[n], out_hbms[n]))
            dkeys = contract_rows(dscores, queries)
            dvalues = contract_rows(probs.astype(BF), out_dir)
            near = pl.ds(start, NEAR)
            total[0:PROMPT, 0:HEAD] += dkeys[0:PROMPT]
            total[0:PROMPT, HEAD:] += dvalues[0:PROMPT]
            total[near, 0:HEAD] += dkeys[PROMPT:]
            total[near, HEAD:] += dvalues[PROMPT:]
        if last:
            result_ref[:, LOCAL : LOCAL + HEAD] = (total[:, 0:HEAD] * FACTOR).astype(BF)
            result_ref[:, LOCAL + HEAD :] = total[:, HEAD:].astype(BF)
            finish(*moved)
            finish(copies.start(result_ref, send_hbm))
        else:
            finish(copies.start(total, total_hbm), *moved)

    return step_kernel


def attention_step(ids, core_arg, seg_row, state, weight, pieces, total, earlier=None):
    count, first, last = len(pieces) // 2, total is None, earlier is not None
    width = pieces[0].shape[1]
    operands = [ids, core_arg, seg_row, *state, weight, *pieces]
    if not first:
        operands.append(total)
    if last:
        operands += earlier
        outs = [((PACK, LOCAL + 2 * HEAD), BF)]
    else:
        outs = [((TOK, LOCAL), BF)] * count + [((PACK, 2 * HEAD), F32)]
    scratch = [
        pltpu.VMEM((count * TOK, 2 * width), BF),
        pltpu.VMEM((2, BLOCKS, HEAD, LOCAL), BF),
        pltpu.VMEM((PACK, HEAD), BF),
        pltpu.VMEM((PACK, HEAD), BF),
        pltpu.VMEM((count, TOK, LOCAL), BF),
        pltpu.VMEM((count, TOK, LOCAL), BF),
        pltpu.VMEM((count, TOK, 2 * GROUP), F32),
        pltpu.VMEM((PACK, 2 * HEAD), F32),
        pltpu.VMEM((PACK, LOCAL + 2 * HEAD) if last else (count, TOK, LOCAL), BF),
        pltpu.SemaphoreType.DMA((32,)),
    ]
    return call(
        make_step_kernel(count, first, last),
        2,
        operands,
        outs,
        scratch,
        in_vmem=(2, 7, 8) if last else (2,),
        flops=count * 1200000000,
        bytes_accessed=12000000,
    )


def start_chunk(copies, pieces, stage, chunk, place):
    width = stage.shape[2]
    columns = pl.ds(pl.multiple_of(place * width, width), width)
    return [
        copies.start(piece.at[:, columns], stage.at[chunk, n * TOK : (n + 1) * TOK, :])
        for n, piece in enumerate(pieces)
    ]


def start_turned(copies, offsets, turned_hbm, turned_ref):
    return [
        copies.start(
            turned_hbm.at[:, k * TOK : (k + 1) * TOK], turned_ref.at[:, n * TOK : (n + 1) * TOK]
        )
        for n, k in enumerate(offsets)
    ]


def make_weight_kernel(offsets, has_early):
    many = len(offsets)

    def weight_kernel(turned_hbm, *refs):
        pieces, refs = refs[:many], refs[many:]
        if has_early:
            early_hbm, out_hbm, turned_ref, stage, out_ref, early_ref, sems = refs
        else:
            out_hbm, turned_ref, stage, out_ref, sems = refs
        copies, moved = Copies(sems), []
        turned = start_turned(copies, offsets, turned_hbm, turned_ref)
        arriving = []
        for c in range(4):
            arriving.append(start_chunk(copies, pieces, stage, c, c))
            if has_early:
                arriving[c].append(copies.start(early_hbm.at[c], early_ref.at[c]))
        finish(*turned)
        for c in range(4):
            finish(*arriving[c])
            sums = jnp.dot(turned_ref[...], stage[c], preferred_element_type=F32)
            if has_early:
                sums = (sums + early_ref[c].astype(F32)).astype(BF)
                for n in range(4):
                    out_ref[4 * c + n] = sums[:, n * HEAD : (n + 1) * HEAD]
                part = pl.ds(4 * c, 4)
            else:
                out_ref[c] = sums.astype(BF)
                part = c
            moved.append(copies.start(out_ref.at[part], out_hbm.at[part]))
        finish(*moved)

    return weight_kernel


def weight_terms(offsets, turned, pieces, early=None):
    width = pieces[0].shape[1] // 4
    operands = [turned, *pieces]
    out = (4, LOCAL, width) if early is None else (BLOCKS, LOCAL, HEAD)
    scratch = [
        pltpu.VMEM((LOCAL, len(offsets) * TOK), BF),
        pltpu.VMEM((4, len(offsets) * TOK, width), BF),
        pltpu.VMEM(out, BF),
    ]
    if early is not None:
        operands.append(early)
        scratch.append(pltpu.VMEM(early.shape, BF))
    return call(
        make_weight_kernel(offsets, early is not None),
        0,
        operands,
        [(out, BF)],
        scratch + [pltpu.SemaphoreType.DMA((48,))],
        in_vmem=[1 + n for n, k in enumerate(offsets) if k == 4],
        flops=len(offsets) * 270000000,
        bytes_accessed=6 << 20,
    )[0]


def make_mine_kernel(offsets):
    many = len(offsets)

    def mine_kernel(place_ref, turned_hbm, early_hbm, arrived_hbm, *refs):
        pieces, out_refs, refs = refs[:many], refs[many : many + 8], refs[many + 8 :]
        turned_ref, stage, early_ref, arrived_ref, half_x, half_y, sems = refs
        copies, moved, arriving = Copies(sems), [], []
        y, x = place_ref[0], place_ref[1]
        turned = start_turned(copies, offsets, turned_hbm, turned_ref)
        for ky in range(4):
            to_y = lax.rem(y + ky, 4)
            arriving.append(start_chunk(copies, pieces, stage, ky, to_y))
            arriving[ky].append(copies.start(early_hbm.at[to_y], early_ref.at[ky]))
            arriving[ky].append(
                copies.start(arrived_hbm.at[pl.ds(to_y * 4, 4)], arrived_ref.at[ky])
            )
        finish(*turned)
        for ky in range(4):
            to_y = lax.rem(y + ky, 4)
            finish(*arriving[ky])
            sums = jnp.dot(turned_ref[...], stage[ky], preferred_element_type=F32)
            sums = sums + early_ref[ky].astype(F32)
            for to_x in range(4):
                both = sums[:, to_x * HEAD : (to_x + 1) * HEAD]
                both = (both + arrived_ref[ky, to_x].astype(F32)).astype(BF)
                half_x[lax.rem(to_x + 4 - x, 4), to_y] = both[0:HALF]
                half_y[ky, to_x] = both[HALF:]
            if ky:
                moved.append(copies.start(half_y.at[ky], out_refs[4 + ky]))
            else:
                out_refs[4][...] = half_y[0]
        for kx in range(1, 4):
            moved.append(copies.start(half_x.at[kx], out_refs[kx]))
        out_refs[0][...] = half_x[0]
        finish(*moved)

    return mine_kernel


def make_middle_kernel(axis):
    def middle_kernel(place_ref, *refs):
        arrived, outs = refs[0:4], refs[4:8]
        for k in range(4):
            at = lax.rem(place_ref[axis] + k, 4)
            outs[k][...] = sum(ref[at].astype(F32) for ref in arrived).astype(outs[k].dtype)

    return middle_kernel


def make_final_kernel(scale):
    def final_kernel(*refs):
        out_ref = refs[8]
        for n in range(2):
            total = sum(ref[...].astype(F32) for ref in refs[4 * n : 4 * n + 4])
            out_ref[:, n * HALF : (n + 1) * HALF] = total.T * scale

    return final_kernel


def call(
    kernel, scalars, operands, outs, scratch=(), in_vmem=(), out_vmem=(), flops=0, bytes_accessed=0
):
    in_specs, placed = [], []
    for n, value in enumerate(operands):
        if n < scalars:
            in_specs.append(SMEM)
        elif n in in_vmem:
            in_specs.append(VMEM)
        else:
            in_specs.append(HBM)
            value = pltpu.with_memory_space_constraint(value, pltpu.HBM)
        placed.append(value)
    return pl.pallas_call(
        kernel,
        out_shape=[
            jax.ShapeDtypeStruct(dims, dtype) if n in out_vmem else pltpu.HBM(dims, dtype)
            for n, (dims, dtype) in enumerate(outs)
        ],
        in_specs=in_specs,
        out_specs=[VMEM if n in out_vmem else HBM for n in range(len(outs))],
        scratch_shapes=list(scratch),
        compiler_params=params(),
        cost_estimate=cost(flops, bytes_accessed),
    )(*placed)


def call_vmem(kernel, scalars, operands, outs, bytes_accessed):
    return pl.pallas_call(
        kernel,
        out_shape=[jax.ShapeDtypeStruct(dims, dtype) for dims, dtype in outs],
        in_specs=[SMEM] * scalars + [VMEM] * (len(operands) - scalars),
        out_specs=[VMEM] * len(outs),
        compiler_params=params(),
        cost_estimate=cost(0, bytes_accessed),
    )(*operands)


def exchange(value):
    return lax.all_to_all(value, "head", split_axis=0, concat_axis=0, tiled=True)


def along_ring(value, shift):
    return lax.ppermute(value, "head", [(i, (i + shift) % RING) for i in range(RING)])


def along_dp(value, dy, dx, dcore):
    pairs = []
    for y in range(4):
        for x in range(4):
            for core in range(2):
                to = (((y + dy) % 4) * 4 + (x + dx) % 4) * 2 + (core + dcore) % 2
                pairs.append(((y * 4 + x) * 2 + core, to))
    return lax.ppermute(value, "dp", pairs)


def shards(query_states, key_states, value_columns, seg_ids, out_grad, out_weight):
    width = out_grad.shape[2]
    half = width // 2
    kv_width = KEY_VALUE_HEADS * HEAD
    joint = (RING, TOK, LOCAL + 2 * HEAD)
    me = lax.axis_index("head").astype(jnp.int32)
    dp = lax.axis_index("dp").astype(jnp.int32)
    me_arg, core_arg = me[None], (dp % 2)[None]
    place = jnp.stack([dp // 8, (dp // 2) % 4])
    weight = out_weight.reshape(BLOCKS, 2, HEAD, LOCAL)

    (packed,) = call(
        pack_kernel,
        0,
        [query_states[0], key_states[0], value_columns[0]],
        [(joint, BF)],
        [
            pltpu.VMEM((TOK, width), BF),
            pltpu.VMEM((TOK, kv_width), BF),
            pltpu.VMEM((TOK, kv_width), BF),
            pltpu.SemaphoreType.DMA((3 + 3 * RING,)),
        ],
        bytes_accessed=3 << 20,
    )
    other0, mine0 = call(
        split_kernel,
        1,
        [core_arg, out_grad[0]],
        [((TOK, half), BF), ((TOK, half), BF)],
        [pltpu.VMEM((TOK, width), BF), pltpu.SemaphoreType.DMA((1 + 2 * BLOCKS,))],
        bytes_accessed=2 << 20,
    )
    up, down = [[other0], [mine0]], [[other0], [mine0]]

    def ring_step(part, *before):
        moved = along_ring(up[part][-1], 1), along_ring(down[part][-1], -1)
        moved, before = lax.optimization_barrier((moved, before))
        up[part].append(moved[0])
        down[part].append(moved[1])
        return before

    pack = exchange(packed).reshape(PACK, LOCAL + 2 * HEAD)
    (pack,) = ring_step(0, pack)
    attn, turned, stat = call(
        forward_kernel,
        1,
        [me_arg, seg_ids, pack],
        [((PACK, LOCAL), BF), ((LOCAL, PACK), BF), ((PACK, 2 * GROUP), F32)],
        [
            pltpu.VMEM((PACK, LOCAL), BF),
            pltpu.VMEM((PACK, HEAD), BF),
            pltpu.VMEM((PACK, HEAD), BF),
            pltpu.VMEM((PACK, LOCAL), BF),
            pltpu.VMEM((LOCAL, PACK), BF),
            pltpu.VMEM((PACK, 2 * GROUP), F32),
            pltpu.SemaphoreType.DMA((6,)),
        ],
        in_vmem=(1,),
        flops=1400000000,
        bytes_accessed=5 << 20,
    )
    (attn,) = ring_step(1, attn)

    def by_offset(part, offsets, far=None):
        found = {0: up[part][0], 4: far}
        for s in range(1, len(up[part])):
            found[s], found[RING - s] = down[part][s], up[part][s]
        return [found[k] for k in offsets]

    near, far_off = (0, 1, 7), (2, 3, 4, 5, 6)
    close, distant = (0, 1, 2, 6, 7), (3, 4, 5)
    other_early = weight_terms(near, turned, by_offset(0, near))
    (other_early,) = ring_step(0, other_early)
    state = (pack, attn, stat)
    query_pieces = [None] * RING

    def both_ways(s):
        ids = [(me + RING - s) % RING, (me + s) % RING]
        return ids, [up[0][s], up[1][s], down[0][s], down[1][s]]

    def pair_step(s, total):
        ids, pieces = both_ways(s)
        query_pieces[RING - s], query_pieces[s], total = attention_step(
            jnp.stack(ids), core_arg, seg_ids, state, weight, pieces, total
        )
        return total

    ids, pieces = both_ways(1)
    query_pieces[0], query_pieces[7], query_pieces[1], total = attention_step(
        jnp.stack([me] + ids), core_arg, seg_ids, state, weight, [other0, mine0] + pieces, None
    )
    (total,) = ring_step(1, total)
    mine_early = weight_terms(close, turned, by_offset(1, close))
    (mine_early,) = ring_step(0, mine_early)
    total = pair_step(2, total)
    other_far = along_ring(up[0][3], 1)
    (total,) = ring_step(1, total)
    mine_far = along_ring(down[1][3], -1)
    total = pair_step(3, total)
    other_far, total = lax.optimization_barrier((other_far, total))

    other = weight_terms(far_off, turned, by_offset(0, far_off, other_far), other_early)
    from_core = along_dp(other, 0, 0, 1)
    mine_far, total, other = lax.optimization_barrier((mine_far, total, other))
    (send,) = attention_step(
        ((me + 4) % RING)[None],
        core_arg,
        seg_ids,
        state,
        weight,
        [other_far, mine_far],
        total,
        [piece for piece in query_pieces if piece is not None],
    )
    turned, send = lax.optimization_barrier((turned, send))
    chunks = (4, len(distant) * TOK, half // 4)
    halves = call(
        make_mine_kernel(distant),
        1,
        [place, turned, mine_early, from_core, *by_offset(1, distant, mine_far)],
        [((4, HALF, HEAD), BF)] * 8,
        [
            pltpu.VMEM((LOCAL, len(distant) * TOK), BF),
            pltpu.VMEM(chunks, BF),
            pltpu.VMEM(mine_early.shape, BF),
            pltpu.VMEM((4, 4, LOCAL, HEAD), BF),
            pltpu.VMEM((4, 4, HALF, HEAD), BF),
            pltpu.VMEM((4, 4, HALF, HEAD), BF),
            pltpu.SemaphoreType.DMA((48,)),
        ],
        in_vmem=[4 + n for n, k in enumerate(distant) if k == 4],
        out_vmem=(0, 4),
        flops=800000000,
        bytes_accessed=9 << 20,
    )
    received = exchange(send.reshape(joint))
    shares = []
    for axis in range(2):
        own_half = halves[4 * axis : 4 * axis + 4]
        steps = [(0, k, 0) if axis == 0 else (k, 0, 0) for k in range(4)]
        arrived = [own_half[0]] + [along_dp(own_half[k], *steps[k]) for k in range(1, 4)]
        middle = call_vmem(
            make_middle_kernel(axis),
            1,
            [place, *arrived],
            [((HALF, HEAD), F32)] + [((HALF, HEAD), BF)] * 3,
            2 << 20,
        )
        steps = [(k, 0, 0) if axis == 0 else (0, k, 0) for k in range(4)]
        shares += [middle[0]] + [along_dp(middle[k], *steps[k]) for k in range(1, 4)]
    query_gradient, key_gradient, value_gradient = call(
        spread_kernel,
        0,
        [received],
        [((TOK, width), BF), ((TOK, kv_width), BF), ((TOK, kv_width), BF)],
        [pltpu.SemaphoreType.DMA((3 * RING,))],
        in_vmem=(0,),
        bytes_accessed=3 << 20,
    )
    shares[7], query_gradient = lax.optimization_barrier((shares[7], query_gradient))
    weight_grad = pl.pallas_call(
        make_final_kernel(1.0 / math.sqrt(lax.axis_size("dp") * PACK)),
        out_shape=jax.ShapeDtypeStruct((HEAD, LOCAL), F32),
        compiler_params=params(),
        cost_estimate=cost(0, 1 << 20),
    )(*shares)
    return (query_gradient[None], key_gradient[None], value_gradient[None], weight_grad)


def solution(mesh):
    in_specs = (
        P("dp", "head", None),
        P("dp", "head", None),
        P("dp", "head", None),
        P("dp", None),
        P("dp", "head", None),
        P(None, "head"),
    )
    out_specs = (
        P("dp", "head", None),
        P("dp", "head", None),
        P("dp", "head", None),
        P("dp", "head"),
    )
    return jax.shard_map(shards, mesh=mesh, in_specs=in_specs, out_specs=out_specs, check_vma=False)
```

```python
import math

import jax
import jax.numpy as jnp
from jax import lax
from jax.experimental import pallas as pl
from jax.experimental.pallas import tpu as pltpu
from jax.sharding import PartitionSpec as P

QUERY_HEADS = 32
KEY_VALUE_HEADS = 8
HEAD = 128
GROUP = QUERY_HEADS // KEY_VALUE_HEADS
TOK = 128
RING = 8
PACK = TOK * RING
BLOCKS = 16
LOCAL = GROUP * HEAD
HALF = LOCAL // 2
PROMPT = 256
NEAR = 384
FACTOR = HEAD ** (-0.5)
MASKED = -1e30
BF = jnp.bfloat16
F32 = jnp.float32
SMEM = pl.BlockSpec(memory_space=pltpu.SMEM)
VMEM = pl.BlockSpec(memory_space=pltpu.VMEM)
HBM = pl.BlockSpec(memory_space=pltpu.HBM)


def params():
    return pltpu.CompilerParams(vmem_limit_bytes=20 * 1024 * 1024)


def cost(flops, bytes_accessed):
    return pl.CostEstimate(flops=flops, bytes_accessed=bytes_accessed, transcendentals=0)


def contract_rows(left, right):
    return lax.dot_general(left, right, (((0,), (0,)), ((), ())), preferred_element_type=F32)


def contract_columns(left, right):
    return lax.dot_general(left, right, (((1,), (1,)), ((), ())), preferred_element_type=F32)


def stacked_heads(block):
    return jnp.concatenate([block[:, h * HEAD : (h + 1) * HEAD] for h in range(GROUP)], axis=0)


def tile_rows(block):
    return pl.ds(pl.multiple_of(block * TOK, TOK), TOK)


def near_start(block):
    return pl.multiple_of(jnp.clip(block - 2, 2, 5) * TOK, TOK)


def window(ref, start):
    return jnp.concatenate([ref[0:PROMPT, :], ref[pl.ds(start, NEAR), :]], axis=0)


def window_bias(block, start, seg_row):
    first = pl.multiple_of(block * TOK, TOK)
    seg_query = seg_row[:, pl.ds(first, TOK)].astype(F32)
    seg_query = jnp.broadcast_to(seg_query, (TOK, TOK)).T[:, 0:1]
    row = first + lax.broadcasted_iota(jnp.int32, (TOK, PROMPT), 0)
    col = lax.broadcasted_iota(jnp.int32, (TOK, PROMPT), 1)
    seg_key = seg_row[:, 0:PROMPT].astype(F32)
    prompt_part = (col <= row) & ((seg_key == 0.0) | (seg_key == seg_query))
    row = first + lax.broadcasted_iota(jnp.int32, (TOK, NEAR), 0)
    col = start + lax.broadcasted_iota(jnp.int32, (TOK, NEAR), 1)
    near_part = (col <= row) & (seg_row[:, pl.ds(start, NEAR)].astype(F32) == seg_query)
    bias = jnp.concatenate(
        [jnp.where(prompt_part, 0.0, MASKED), jnp.where(near_part, 0.0, MASKED)], axis=1
    )
    return jnp.concatenate([bias] * GROUP, axis=0)


class Copies:
    def __init__(self, sems):
        self.sems, self.used = sems, 0

    def start(self, source, target):
        copy = pltpu.make_async_copy(source, target, self.sems.at[self.used])
        self.used += 1
        copy.start()
        return copy


def finish(*copies):
    for copy in copies:
        copy.wait()


def pack_kernel(query_hbm, key_hbm, value_hbm, out_hbm, query_ref, key_ref, value_ref, sems):
    copies, pending, begin = Copies(sems), [], LOCAL
    arriving = [
        copies.start(
            query_hbm.at[:, t * LOCAL : (t + 1) * LOCAL],
            query_ref.at[:, t * LOCAL : (t + 1) * LOCAL],
        )
        for t in range(RING)
    ]
    narrow = ((copies.start(key_hbm, key_ref), key_ref), (copies.start(value_hbm, value_ref), value_ref))
    for t in range(RING):
        arriving[t].wait()
        source = query_ref.at[:, t * LOCAL : (t + 1) * LOCAL]
        pending.append(copies.start(source, out_hbm.at[t, :, 0:LOCAL]))
    for copy, ref in narrow:
        copy.wait()
        for t in range(RING):
            pending.append(
                copies.start(
                    ref.at[:, t * HEAD : (t + 1) * HEAD], out_hbm.at[t, :, begin : begin + HEAD]
                )
            )
        begin += HEAD
    finish(*pending)


def split_kernel(core_ref, grad_hbm, other_hbm, mine_hbm, held, sems):
    copies, core, pending = Copies(sems), core_ref[0], []
    arriving = []
    for n in range(4):
        part = pl.ds(n * 8 * HEAD, 8 * HEAD)
        arriving.append(copies.start(grad_hbm.at[:, part], held.at[:, part]))
    for n in range(BLOCKS):
        if n % 4 == 0:
            arriving[n // 4].wait()
        for target, side in ((other_hbm, 1 - core), (mine_hbm, core)):
            source = pl.ds(pl.multiple_of((2 * n + side) * HEAD, HEAD), HEAD)
            pending.append(
                copies.start(held.at[:, source], target.at[:, n * HEAD : (n + 1) * HEAD])
            )
    finish(*pending)


def spread_kernel(in_ref, query_hbm, key_hbm, value_hbm, sems):
    copies, pending = Copies(sems), []
    for t in range(RING):
        begin = 0
        for target, width in ((query_hbm, LOCAL), (key_hbm, HEAD), (value_hbm, HEAD)):
            pending.append(
                copies.start(
                    in_ref.at[t, :, begin : begin + width],
                    target.at[:, t * width : (t + 1) * width],
                )
            )
            begin += width
    finish(*pending)


def forward_kernel(me_ref, seg_row, pack_hbm, attn_hbm, turned_hbm, stat_hbm, *scratch):
    query_ref, key_ref, value_ref, attn_ref, turned_ref, stat_ref, sems = scratch
    copies, me = Copies(sems), me_ref[0]
    finish(
        copies.start(pack_hbm.at[:, 0:LOCAL], query_ref),
        copies.start(pack_hbm.at[:, LOCAL : LOCAL + HEAD], key_ref),
        copies.start(pack_hbm.at[:, LOCAL + HEAD :], value_ref),
    )

    def one_block(block, carry):
        start = near_start(block)
        rows_of = tile_rows(block)
        queries = stacked_heads(query_ref[rows_of, :])
        scores = contract_columns(queries, window(key_ref, start)) * FACTOR
        scores = scores + window_bias(block, start, seg_row)
        row_max = jnp.max(scores, axis=1, keepdims=True)
        terms = jnp.exp(scores - row_max)
        inverse = 1.0 / jnp.sum(terms, axis=1, keepdims=True)
        probs = (terms * inverse).astype(BF)
        attn = jnp.dot(probs, window(value_ref, start), preferred_element_type=F32)
        turned = tile_rows(lax.rem(block + RING - me, RING))
        for h in range(GROUP):
            rows = slice(h * TOK, (h + 1) * TOK)
            attn_ref[rows_of, rows] = attn[rows].astype(BF)
            turned_ref[rows, turned] = attn[rows].T.astype(BF)
        stat_ref[rows_of, :] = jnp.concatenate(
            [row_max[h * TOK : (h + 1) * TOK] for h in range(GROUP)]
            + [inverse[h * TOK : (h + 1) * TOK] for h in range(GROUP)],
            axis=1,
        )
        return carry

    lax.fori_loop(0, RING, one_block, 0, unroll=4)
    finish(
        copies.start(attn_ref, attn_hbm),
        copies.start(turned_ref, turned_hbm),
        copies.start(stat_ref, stat_hbm),
    )


def make_step_kernel(count, first, last):
    def step_kernel(*refs):
        id_ref, core_ref, seg_row, pack_hbm, attn_hbm, stat_hbm, weight_ref = refs[:7]
        weight_hbm = weight_ref
        refs = refs[7:]
        pieces, refs = refs[: 2 * count], refs[2 * count :]
        if not first:
            total_in, refs = refs[0], refs[2:]
        send_hbm, refs = refs[0], refs[1:]
        total, refs = refs[0], refs[1:]
        if not last:
            weight_ref, refs = refs[0], refs[1:]
        grad_ref, key_ref, value_ref, query_ref, attn_ref, stat_ref = refs[:6]
        result_ref, cast_ref, sems = refs[6:]
        copies, core = Copies(sems), core_ref[0]
        blocks = [id_ref[n] for n in range(count)]
        width = pieces[0].shape[1]
        need_scores, need_grads, need_attn, moved = [], ([], []), [], []
        need_scores.append(copies.start(pack_hbm.at[:, LOCAL : LOCAL + HEAD], key_ref))
        for n, block in enumerate(blocks):
            rows = tile_rows(block)
            need_scores.append(copies.start(pack_hbm.at[rows, 0:LOCAL], query_ref.at[n]))
            need_scores.append(copies.start(stat_hbm.at[rows, :], stat_ref.at[n]))
        for part, side in enumerate((1 - core, core)):
            if not last:
                need_grads[part].append(
                    copies.start(weight_hbm.at[:, side], weight_ref.at[part])
                )
            for n in range(count):
                need_grads[part].append(
                    copies.start(
                        pieces[2 * n + part],
                        grad_ref.at[
                            n * TOK : (n + 1) * TOK, part * width : (part + 1) * width
                        ],
                    )
                )
        need_attn.append(copies.start(pack_hbm.at[:, LOCAL + HEAD :], value_ref))
        for n, block in enumerate(blocks):
            need_attn.append(copies.start(attn_hbm.at[tile_rows(block), :], attn_ref.at[n]))
        finish(*need_scores)
        all_probs = []
        for n, block in enumerate(blocks):
            start = near_start(block)
            stat = stat_ref[n]
            row_max = jnp.concatenate([stat[:, h : h + 1] for h in range(GROUP)], axis=0)
            inverse = jnp.concatenate(
                [stat[:, GROUP + h : GROUP + h + 1] for h in range(GROUP)], axis=0
            )
            queries = stacked_heads(query_ref[n])
            scores = contract_columns(queries, window(key_ref, start)) * FACTOR
            scores = scores + window_bias(block, start, seg_row)
            all_probs.append(jnp.exp(scores - row_max) * inverse)
        direction = 0.0
        for part in range(2):
            finish(*need_grads[part])
            direction = direction + jnp.dot(
                grad_ref[:, part * width : (part + 1) * width],
                weight_ref[part].reshape(width, LOCAL),
                preferred_element_type=F32,
            )
        direction = direction.astype(BF)
        finish(*need_attn)
        total[...] = jnp.zeros_like(total) if first else total_in[...]
        for n, block in enumerate(blocks):
            start = near_start(block)
            probs = all_probs[n]
            keys = window(key_ref, start)
            queries = stacked_heads(query_ref[n])
            out_dir = stacked_heads(direction[n * TOK : (n + 1) * TOK])
            attn = stacked_heads(attn_ref[n])
            delta = jnp.sum(out_dir.astype(F32) * attn.astype(F32), axis=1, keepdims=True)
            dprobs = contract_columns(out_dir, window(value_ref, start))
            dscores = (probs * (dprobs - delta)).astype(BF)
            dquery = (jnp.dot(dscores, keys, preferred_element_type=F32) * FACTOR).astype(BF)
            for h in range(GROUP):
                columns = slice(h * HEAD, (h + 1) * HEAD)
                result_ref[n, :, columns] = dquery[h * TOK : (h + 1) * TOK]
            target = send_hbm.at[tile_rows(block), 0:LOCAL]
            moved.append(copies.start(result_ref.at[n], target))
            dkeys = contract_rows(dscores, queries)
            dvalues = contract_rows(probs.astype(BF), out_dir)
            near = pl.ds(start, NEAR)
            total[0:PROMPT, 0:HEAD] += dkeys[0:PROMPT]
            total[0:PROMPT, HEAD:] += dvalues[0:PROMPT]
            total[near, 0:HEAD] += dkeys[PROMPT:]
            total[near, HEAD:] += dvalues[PROMPT:]
        if last:
            cast_ref[:, 0:HEAD] = (total[:, 0:HEAD] * FACTOR).astype(BF)
            cast_ref[:, HEAD:] = total[:, HEAD:].astype(BF)
            moved.append(copies.start(cast_ref, send_hbm.at[:, LOCAL:]))
        finish(*moved)

    return step_kernel


def attention_step(
    ids, core_arg, seg_row, state, weight, pieces, carried, last=False, keep=False
):
    count, first = len(pieces) // 2, carried is None
    width = pieces[0].shape[1]
    operands = [ids, core_arg, seg_row, *state, weight, *pieces]
    outs = [((PACK, LOCAL + 2 * HEAD), BF)]
    in_vmem, out_vmem, aliases, scratch = [2], (1, 2), {}, []
    if not first:
        operands += carried
        in_vmem.append(len(operands) - 2)
        aliases = {len(operands) - 1: 0}
    if last:
        in_vmem += [6, 7, 8]
        scratch.append(pltpu.VMEM((PACK, 2 * HEAD), F32))
    else:
        outs.append(((PACK, 2 * HEAD), F32))
        if not first:
            aliases[len(operands) - 2] = 1
        held = (2, BLOCKS, HEAD, LOCAL)
        if keep:
            outs.append((held, BF))
        else:
            scratch.append(pltpu.VMEM(held, BF))
    scratch += [
        pltpu.VMEM((count * TOK, 2 * width), BF),
        pltpu.VMEM((PACK, HEAD), BF),
        pltpu.VMEM((PACK, HEAD), BF),
        pltpu.VMEM((count, TOK, LOCAL), BF),
        pltpu.VMEM((count, TOK, LOCAL), BF),
        pltpu.VMEM((count, TOK, 2 * GROUP), F32),
        pltpu.VMEM((count, TOK, LOCAL), BF),
        pltpu.VMEM((PACK, 2 * HEAD), BF),
        pltpu.SemaphoreType.DMA((32,)),
    ]
    return call(
        make_step_kernel(count, first, last),
        2,
        operands,
        outs,
        scratch,
        in_vmem=in_vmem,
        out_vmem=out_vmem,
        aliases=aliases,
        flops=count * 1200000000,
        bytes_accessed=12000000,
    )


def start_chunk(copies, pieces, stage, chunk, place):
    width = stage.shape[2]
    columns = pl.ds(pl.multiple_of(place * width, width), width)
    return [
        copies.start(piece.at[:, columns], stage.at[chunk, n * TOK : (n + 1) * TOK, :])
        for n, piece in enumerate(pieces)
    ]


def start_turned(copies, offsets, turned_hbm, turned_ref):
    return [
        copies.start(
            turned_hbm.at[:, k * TOK : (k + 1) * TOK], turned_ref.at[:, n * TOK : (n + 1) * TOK]
        )
        for n, k in enumerate(offsets)
    ]


def make_weight_kernel(offsets, has_early):
    many = len(offsets)

    def weight_kernel(turned_hbm, *refs):
        pieces, refs = refs[:many], refs[many:]
        if has_early:
            early_hbm, out_hbm, turned_ref, stage, out_ref, early_ref, sems = refs
        else:
            out_hbm, turned_ref, stage, out_ref, sems = refs
        copies, moved = Copies(sems), []
        turned = start_turned(copies, offsets, turned_hbm, turned_ref)
        arriving = []
        for c in range(4):
            arriving.append(start_chunk(copies, pieces, stage, c, c))
            if has_early:
                arriving[c].append(copies.start(early_hbm.at[c], early_ref.at[c]))
        finish(*turned)
        for c in range(4):
            finish(*arriving[c])
            sums = jnp.dot(turned_ref[...], stage[c], preferred_element_type=F32)
            if has_early:
                sums = (sums + early_ref[c].astype(F32)).astype(BF)
                for n in range(4):
                    out_ref[4 * c + n] = sums[:, n * HEAD : (n + 1) * HEAD]
                part = pl.ds(4 * c, 4)
            else:
                out_ref[c] = sums.astype(BF)
                part = c
            moved.append(copies.start(out_ref.at[part], out_hbm.at[part]))
        finish(*moved)

    return weight_kernel


def weight_terms(offsets, turned, pieces, early=None):
    width = pieces[0].shape[1] // 4
    operands = [turned, *pieces]
    out = (4, LOCAL, width) if early is None else (BLOCKS, LOCAL, HEAD)
    scratch = [
        pltpu.VMEM((LOCAL, len(offsets) * TOK), BF),
        pltpu.VMEM((4, len(offsets) * TOK, width), BF),
        pltpu.VMEM(out, BF),
    ]
    if early is not None:
        operands.append(early)
        scratch.append(pltpu.VMEM(early.shape, BF))
    return call(
        make_weight_kernel(offsets, early is not None),
        0,
        operands,
        [(out, BF)],
        scratch + [pltpu.SemaphoreType.DMA((48,))],
        in_vmem=[1 + n for n, k in enumerate(offsets) if k == 4],
        flops=len(offsets) * 270000000,
        bytes_accessed=6 << 20,
    )[0]


def make_mine_kernel(offsets):
    many = len(offsets)

    def mine_kernel(place_ref, turned_hbm, early_hbm, arrived_hbm, *refs):
        pieces, out_refs, refs = refs[:many], refs[many : many + 8], refs[many + 8 :]
        turned_ref, stage, early_ref, arrived_ref, half_x, half_y, sems = refs
        copies, moved, arriving = Copies(sems), [], []
        y, x = place_ref[0], place_ref[1]
        turned = start_turned(copies, offsets, turned_hbm, turned_ref)
        for ky in range(4):
            to_y = lax.rem(y + ky, 4)
            arriving.append(start_chunk(copies, pieces, stage, ky, to_y))
            arriving[ky].append(copies.start(early_hbm.at[to_y], early_ref.at[ky]))
            arriving[ky].append(
                copies.start(arrived_hbm.at[pl.ds(to_y * 4, 4)], arrived_ref.at[ky])
            )
        finish(*turned)
        for ky in range(4):
            to_y = lax.rem(y + ky, 4)
            finish(*arriving[ky])
            sums = jnp.dot(turned_ref[...], stage[ky], preferred_element_type=F32)
            sums = sums + early_ref[ky].astype(F32)
            for to_x in range(4):
                both = sums[:, to_x * HEAD : (to_x + 1) * HEAD]
                both = (both + arrived_ref[ky, to_x].astype(F32)).astype(BF)
                half_x[lax.rem(to_x + 4 - x, 4), to_y] = both[0:HALF]
                half_y[ky, to_x] = both[HALF:]
            if ky:
                moved.append(copies.start(half_y.at[ky], out_refs[4 + ky]))
            else:
                out_refs[4][...] = half_y[0]
        for kx in range(1, 4):
            moved.append(copies.start(half_x.at[kx], out_refs[kx]))
        out_refs[0][...] = half_x[0]
        finish(*moved)

    return mine_kernel


def make_middle_kernel(axis):
    def middle_kernel(place_ref, *refs):
        arrived, outs = refs[0:4], refs[4:8]
        for k in range(4):
            at = lax.rem(place_ref[axis] + k, 4)
            outs[k][...] = sum(ref[at].astype(F32) for ref in arrived).astype(outs[k].dtype)

    return middle_kernel


def make_final_kernel(scale):
    def final_kernel(*refs):
        out_ref = refs[8]
        for n in range(2):
            total = sum(ref[...].astype(F32) for ref in refs[4 * n : 4 * n + 4])
            out_ref[:, n * HALF : (n + 1) * HALF] = total.T * scale

    return final_kernel


def call(
    kernel,
    scalars,
    operands,
    outs,
    scratch=(),
    in_vmem=(),
    out_vmem=(),
    aliases=None,
    flops=0,
    bytes_accessed=0,
):
    in_specs, placed = [], []
    for n, value in enumerate(operands):
        if n < scalars:
            in_specs.append(SMEM)
        elif n in in_vmem:
            in_specs.append(VMEM)
        else:
            in_specs.append(HBM)
            value = pltpu.with_memory_space_constraint(value, pltpu.HBM)
        placed.append(value)
    return pl.pallas_call(
        kernel,
        out_shape=[
            jax.ShapeDtypeStruct(dims, dtype) if n in out_vmem else pltpu.HBM(dims, dtype)
            for n, (dims, dtype) in enumerate(outs)
        ],
        in_specs=in_specs,
        out_specs=[VMEM if n in out_vmem else HBM for n in range(len(outs))],
        scratch_shapes=list(scratch),
        input_output_aliases=aliases or {},
        compiler_params=params(),
        cost_estimate=cost(flops, bytes_accessed),
    )(*placed)


def call_vmem(kernel, scalars, operands, outs, bytes_accessed):
    return pl.pallas_call(
        kernel,
        out_shape=[jax.ShapeDtypeStruct(dims, dtype) for dims, dtype in outs],
        in_specs=[SMEM] * scalars + [VMEM] * (len(operands) - scalars),
        out_specs=[VMEM] * len(outs),
        compiler_params=params(),
        cost_estimate=cost(0, bytes_accessed),
    )(*operands)


def exchange(value):
    return lax.all_to_all(value, "head", split_axis=0, concat_axis=0, tiled=True)


def along_ring(value, shift):
    return lax.ppermute(value, "head", [(i, (i + shift) % RING) for i in range(RING)])


def along_dp(value, dy, dx, dcore):
    pairs = []
    for y in range(4):
        for x in range(4):
            for core in range(2):
                to = (((y + dy) % 4) * 4 + (x + dx) % 4) * 2 + (core + dcore) % 2
                pairs.append(((y * 4 + x) * 2 + core, to))
    return lax.ppermute(value, "dp", pairs)


def shards(query_states, key_states, value_columns, seg_ids, out_grad, out_weight):
    width = out_grad.shape[2]
    half = width // 2
    kv_width = KEY_VALUE_HEADS * HEAD
    joint = (RING, TOK, LOCAL + 2 * HEAD)
    me = lax.axis_index("head").astype(jnp.int32)
    dp = lax.axis_index("dp").astype(jnp.int32)
    me_arg, core_arg = me[None], (dp % 2)[None]
    place = jnp.stack([dp // 8, (dp // 2) % 4])
    weight_blocks = out_weight.reshape(BLOCKS, 2, HEAD, LOCAL)

    (packed,) = call(
        pack_kernel,
        0,
        [query_states[0], key_states[0], value_columns[0]],
        [(joint, BF)],
        [
            pltpu.VMEM((TOK, width), BF),
            pltpu.VMEM((TOK, kv_width), BF),
            pltpu.VMEM((TOK, kv_width), BF),
            pltpu.SemaphoreType.DMA((2 + 4 * RING,)),
        ],
        bytes_accessed=3 << 20,
    )
    other0, mine0 = call(
        split_kernel,
        1,
        [core_arg, out_grad[0]],
        [((TOK, half), BF), ((TOK, half), BF)],
        [pltpu.VMEM((TOK, width), BF), pltpu.SemaphoreType.DMA((4 + 2 * BLOCKS,))],
        bytes_accessed=2 << 20,
    )
    up, down = [[other0], [mine0]], [[other0], [mine0]]

    def ring_step(part, *before):
        moved = along_ring(up[part][-1], 1), along_ring(down[part][-1], -1)
        moved, before = lax.optimization_barrier((moved, before))
        up[part].append(moved[0])
        down[part].append(moved[1])
        return before

    pack = exchange(packed).reshape(PACK, LOCAL + 2 * HEAD)
    (pack,) = ring_step(0, pack)
    attn, turned, stat = call(
        forward_kernel,
        1,
        [me_arg, seg_ids, pack],
        [((PACK, LOCAL), BF), ((LOCAL, PACK), BF), ((PACK, 2 * GROUP), F32)],
        [
            pltpu.VMEM((PACK, LOCAL), BF),
            pltpu.VMEM((PACK, HEAD), BF),
            pltpu.VMEM((PACK, HEAD), BF),
            pltpu.VMEM((PACK, LOCAL), BF),
            pltpu.VMEM((LOCAL, PACK), BF),
            pltpu.VMEM((PACK, 2 * GROUP), F32),
            pltpu.SemaphoreType.DMA((6,)),
        ],
        in_vmem=(1,),
        flops=1400000000,
        bytes_accessed=5 << 20,
    )
    (attn,) = ring_step(1, attn)

    def by_offset(part, offsets, far=None):
        found = {0: up[part][0], 4: far}
        for s in range(1, len(up[part])):
            found[s], found[RING - s] = down[part][s], up[part][s]
        return [found[k] for k in offsets]

    near, far_off = (0, 1, 7), (2, 3, 4, 5, 6)
    close, distant = (0, 1, 2, 6, 7), (3, 4, 5)
    other_early = weight_terms(near, turned, by_offset(0, near))
    (other_early,) = ring_step(0, other_early)
    state = (pack, attn, stat)

    def both_ways(s):
        ids = [(me + RING - s) % RING, (me + s) % RING]
        return ids, [up[0][s], up[1][s], down[0][s], down[1][s]]

    def step(ids, pieces, carried, keep=False):
        send, total, *weight = attention_step(
            jnp.stack(ids), core_arg, seg_ids, state, weight_blocks, pieces, carried, keep=keep
        )
        return [total, send] + weight

    ids, pieces = both_ways(1)
    total, send = step([me] + ids, [other0, mine0] + pieces, None)
    (total,) = ring_step(1, total)
    mine_early = weight_terms(close, turned, by_offset(1, close))
    (mine_early,) = ring_step(0, mine_early)
    total, send = step(*both_ways(2), [total, send])
    other_far = along_ring(up[0][3], 1)
    (total,) = ring_step(1, total)
    mine_far = along_ring(down[1][3], -1)
    total, send, weight = step(*both_ways(3), [total, send], keep=True)
    other_far, total = lax.optimization_barrier((other_far, total))

    other = weight_terms(far_off, turned, by_offset(0, far_off, other_far), other_early)
    from_core = along_dp(other, 0, 0, 1)
    mine_far, total, other = lax.optimization_barrier((mine_far, total, other))
    (send,) = attention_step(
        ((me + 4) % RING)[None],
        core_arg,
        seg_ids,
        state,
        weight,
        [other_far, mine_far],
        [total, send],
        last=True,
    )
    turned, send = lax.optimization_barrier((turned, send))
    chunks = (4, len(distant) * TOK, half // 4)
    halves = call(
        make_mine_kernel(distant),
        1,
        [place, turned, mine_early, from_core, *by_offset(1, distant, mine_far)],
        [((4, HALF, HEAD), BF)] * 8,
        [
            pltpu.VMEM((LOCAL, len(distant) * TOK), BF),
            pltpu.VMEM(chunks, BF),
            pltpu.VMEM(mine_early.shape, BF),
            pltpu.VMEM((4, 4, LOCAL, HEAD), BF),
            pltpu.VMEM((4, 4, HALF, HEAD), BF),
            pltpu.VMEM((4, 4, HALF, HEAD), BF),
            pltpu.SemaphoreType.DMA((48,)),
        ],
        in_vmem=[4 + n for n, k in enumerate(distant) if k == 4],
        out_vmem=(0, 4),
        flops=800000000,
        bytes_accessed=9 << 20,
    )
    received = exchange(send.reshape(joint))
    shares = []
    for axis in range(2):
        own_half = halves[4 * axis : 4 * axis + 4]
        steps = [(0, k, 0) if axis == 0 else (k, 0, 0) for k in range(4)]
        arrived = [own_half[0]] + [along_dp(own_half[k], *steps[k]) for k in range(1, 4)]
        middle = call_vmem(
            make_middle_kernel(axis),
            1,
            [place, *arrived],
            [((HALF, HEAD), F32)] + [((HALF, HEAD), BF)] * 3,
            2 << 20,
        )
        steps = [(k, 0, 0) if axis == 0 else (0, k, 0) for k in range(4)]
        shares += [middle[0]] + [along_dp(middle[k], *steps[k]) for k in range(1, 4)]
    query_gradient, key_gradient, value_gradient = call(
        spread_kernel,
        0,
        [received],
        [((TOK, width), BF), ((TOK, kv_width), BF), ((TOK, kv_width), BF)],
        [pltpu.SemaphoreType.DMA((3 * RING,))],
        in_vmem=(0,),
        bytes_accessed=3 << 20,
    )
    shares[7], query_gradient = lax.optimization_barrier((shares[7], query_gradient))
    weight_grad = pl.pallas_call(
        make_final_kernel(1.0 / math.sqrt(lax.axis_size("dp") * PACK)),
        out_shape=jax.ShapeDtypeStruct((HEAD, LOCAL), F32),
        compiler_params=params(),
        cost_estimate=cost(0, 1 << 20),
    )(*shares)
    return (query_gradient[None], key_gradient[None], value_gradient[None], weight_grad)


def solution(mesh):
    in_specs = (
        P("dp", "head", None),
        P("dp", "head", None),
        P("dp", "head", None),
        P("dp", None),
        P("dp", "head", None),
        P(None, "head"),
    )
    out_specs = (
        P("dp", "head", None),
        P("dp", "head", None),
        P("dp", "head", None),
        P("dp", "head"),
    )
    return jax.shard_map(shards, mesh=mesh, in_specs=in_specs, out_specs=out_specs, check_vma=False)
```

```python
import math

import jax
import jax.numpy as jnp
from jax import lax
from jax.experimental import pallas as pl
from jax.experimental.pallas import tpu as pltpu
from jax.sharding import PartitionSpec as P

QUERY_HEADS = 32
KEY_VALUE_HEADS = 8
HEAD = 128
GROUP = QUERY_HEADS // KEY_VALUE_HEADS
TOK = 128
RING = 8
PACK = TOK * RING
BLOCKS = 16
LOCAL = GROUP * HEAD
X_ROWS = 224
SHARES = (X_ROWS, LOCAL - X_ROWS)
PROMPT = 256
NEAR = 384
FACTOR = HEAD ** (-0.5)
MASKED = -1e30
BF = jnp.bfloat16
F32 = jnp.float32
SMEM = pl.BlockSpec(memory_space=pltpu.SMEM)
VMEM = pl.BlockSpec(memory_space=pltpu.VMEM)
HBM = pl.BlockSpec(memory_space=pltpu.HBM)


def params():
    return pltpu.CompilerParams(vmem_limit_bytes=20 * 1024 * 1024)


def cost(flops, bytes_accessed):
    return pl.CostEstimate(flops=flops, bytes_accessed=bytes_accessed, transcendentals=0)


def contract_rows(left, right):
    return lax.dot_general(left, right, (((0,), (0,)), ((), ())), preferred_element_type=F32)


def contract_columns(left, right):
    return lax.dot_general(left, right, (((1,), (1,)), ((), ())), preferred_element_type=F32)


def stacked_heads(block):
    return jnp.concatenate([block[:, h * HEAD : (h + 1) * HEAD] for h in range(GROUP)], axis=0)


def tile_rows(block):
    return pl.ds(pl.multiple_of(block * TOK, TOK), TOK)


def near_start(block):
    return pl.multiple_of(jnp.clip(block - 2, 2, 5) * TOK, TOK)


def window(ref, start):
    return jnp.concatenate([ref[0:PROMPT, :], ref[pl.ds(start, NEAR), :]], axis=0)


def window_bias(block, start, seg_row):
    first = pl.multiple_of(block * TOK, TOK)
    seg_query = seg_row[:, pl.ds(first, TOK)].astype(F32)
    seg_query = jnp.broadcast_to(seg_query, (TOK, TOK)).T[:, 0:1]
    row = first + lax.broadcasted_iota(jnp.int32, (TOK, PROMPT), 0)
    col = lax.broadcasted_iota(jnp.int32, (TOK, PROMPT), 1)
    seg_key = seg_row[:, 0:PROMPT].astype(F32)
    prompt_part = (col <= row) & ((seg_key == 0.0) | (seg_key == seg_query))
    row = first + lax.broadcasted_iota(jnp.int32, (TOK, NEAR), 0)
    col = start + lax.broadcasted_iota(jnp.int32, (TOK, NEAR), 1)
    near_part = (col <= row) & (seg_row[:, pl.ds(start, NEAR)].astype(F32) == seg_query)
    bias = jnp.concatenate(
        [jnp.where(prompt_part, 0.0, MASKED), jnp.where(near_part, 0.0, MASKED)], axis=1
    )
    return jnp.concatenate([bias] * GROUP, axis=0)


class Copies:
    def __init__(self, sems):
        self.sems, self.used = sems, 0

    def start(self, source, target):
        copy = pltpu.make_async_copy(source, target, self.sems.at[self.used])
        self.used += 1
        copy.start()
        return copy


def finish(*copies):
    for copy in copies:
        copy.wait()


def pack_kernel(query_hbm, key_hbm, value_hbm, out_hbm, query_ref, key_ref, value_ref, sems):
    copies, pending, begin = Copies(sems), [], LOCAL
    arriving = [
        copies.start(
            query_hbm.at[:, t * LOCAL : (t + 1) * LOCAL],
            query_ref.at[:, t * LOCAL : (t + 1) * LOCAL],
        )
        for t in range(RING)
    ]
    narrow = ((copies.start(key_hbm, key_ref), key_ref), (copies.start(value_hbm, value_ref), value_ref))
    for t in range(RING):
        arriving[t].wait()
        source = query_ref.at[:, t * LOCAL : (t + 1) * LOCAL]
        pending.append(copies.start(source, out_hbm.at[t, :, 0:LOCAL]))
    for copy, ref in narrow:
        copy.wait()
        for t in range(RING):
            pending.append(
                copies.start(
                    ref.at[:, t * HEAD : (t + 1) * HEAD], out_hbm.at[t, :, begin : begin + HEAD]
                )
            )
        begin += HEAD
    finish(*pending)


def split_kernel(core_ref, grad_hbm, other_hbm, mine_hbm, held, sems):
    copies, core, pending = Copies(sems), core_ref[0], []
    arriving = []
    for n in range(4):
        part = pl.ds(n * 8 * HEAD, 8 * HEAD)
        arriving.append(copies.start(grad_hbm.at[:, part], held.at[:, part]))
    for n in range(BLOCKS):
        if n % 4 == 0:
            arriving[n // 4].wait()
        for target, side in ((other_hbm, 1 - core), (mine_hbm, core)):
            source = pl.ds(pl.multiple_of((2 * n + side) * HEAD, HEAD), HEAD)
            pending.append(
                copies.start(held.at[:, source], target.at[:, n * HEAD : (n + 1) * HEAD])
            )
    finish(*pending)


def spread_kernel(in_ref, query_hbm, key_hbm, value_hbm, sems):
    copies, pending = Copies(sems), []
    for t in range(RING):
        begin = 0
        for target, width in ((query_hbm, LOCAL), (key_hbm, HEAD), (value_hbm, HEAD)):
            pending.append(
                copies.start(
                    in_ref.at[t, :, begin : begin + width],
                    target.at[:, t * width : (t + 1) * width],
                )
            )
            begin += width
    finish(*pending)


def forward_kernel(me_ref, seg_row, pack_hbm, attn_hbm, turned_hbm, stat_hbm, *scratch):
    query_ref, key_ref, value_ref, attn_ref, turned_ref, stat_ref, sems = scratch
    copies, me = Copies(sems), me_ref[0]
    finish(
        copies.start(pack_hbm.at[:, 0:LOCAL], query_ref),
        copies.start(pack_hbm.at[:, LOCAL : LOCAL + HEAD], key_ref),
        copies.start(pack_hbm.at[:, LOCAL + HEAD :], value_ref),
    )

    def one_block(block, carry):
        start = near_start(block)
        rows_of = tile_rows(block)
        queries = stacked_heads(query_ref[rows_of, :])
        scores = contract_columns(queries, window(key_ref, start)) * FACTOR
        scores = scores + window_bias(block, start, seg_row)
        row_max = jnp.max(scores, axis=1, keepdims=True)
        terms = jnp.exp(scores - row_max)
        inverse = 1.0 / jnp.sum(terms, axis=1, keepdims=True)
        probs = (terms * inverse).astype(BF)
        attn = jnp.dot(probs, window(value_ref, start), preferred_element_type=F32)
        turned = tile_rows(lax.rem(block + RING - me, RING))
        for h in range(GROUP):
            rows = slice(h * TOK, (h + 1) * TOK)
            attn_ref[rows_of, rows] = attn[rows].astype(BF)
            turned_ref[rows, turned] = attn[rows].T.astype(BF)
        stat_ref[rows_of, :] = jnp.concatenate(
            [row_max[h * TOK : (h + 1) * TOK] for h in range(GROUP)]
            + [inverse[h * TOK : (h + 1) * TOK] for h in range(GROUP)],
            axis=1,
        )
        return carry

    lax.fori_loop(0, RING, one_block, 0, unroll=4)
    finish(
        copies.start(attn_ref, attn_hbm),
        copies.start(turned_ref, turned_hbm),
        copies.start(stat_ref, stat_hbm),
    )


def make_step_kernel(count, first, last):
    def step_kernel(*refs):
        id_ref, core_ref, seg_row, pack_hbm, attn_hbm, stat_hbm, weight_ref = refs[:7]
        weight_hbm = weight_ref
        refs = refs[7:]
        pieces, refs = refs[: 2 * count], refs[2 * count :]
        if not first:
            total_in, refs = refs[0], refs[2:]
        send_hbm, refs = refs[0], refs[1:]
        total, refs = refs[0], refs[1:]
        if not last:
            weight_ref, refs = refs[0], refs[1:]
        grad_ref, key_ref, value_ref, query_ref, attn_ref, stat_ref = refs[:6]
        result_ref, cast_ref, sems = refs[6:]
        copies, core = Copies(sems), core_ref[0]
        blocks = [id_ref[n] for n in range(count)]
        width = pieces[0].shape[1]
        need_scores, need_grads, need_attn, moved = [], ([], []), [], []
        need_scores.append(copies.start(pack_hbm.at[:, LOCAL : LOCAL + HEAD], key_ref))
        for n, block in enumerate(blocks):
            rows = tile_rows(block)
            need_scores.append(copies.start(pack_hbm.at[rows, 0:LOCAL], query_ref.at[n]))
            need_scores.append(copies.start(stat_hbm.at[rows, :], stat_ref.at[n]))
        for part, side in enumerate((1 - core, core)):
            if not last:
                need_grads[part].append(
                    copies.start(weight_hbm.at[:, side], weight_ref.at[part])
                )
            for n in range(count):
                need_grads[part].append(
                    copies.start(
                        pieces[2 * n + part],
                        grad_ref.at[
                            n * TOK : (n + 1) * TOK, part * width : (part + 1) * width
                        ],
                    )
                )
        need_attn.append(copies.start(pack_hbm.at[:, LOCAL + HEAD :], value_ref))
        for n, block in enumerate(blocks):
            need_attn.append(copies.start(attn_hbm.at[tile_rows(block), :], attn_ref.at[n]))
        finish(*need_scores)
        all_probs = []
        for n, block in enumerate(blocks):
            start = near_start(block)
            stat = stat_ref[n]
            row_max = jnp.concatenate([stat[:, h : h + 1] for h in range(GROUP)], axis=0)
            inverse = jnp.concatenate(
                [stat[:, GROUP + h : GROUP + h + 1] for h in range(GROUP)], axis=0
            )
            queries = stacked_heads(query_ref[n])
            scores = contract_columns(queries, window(key_ref, start)) * FACTOR
            scores = scores + window_bias(block, start, seg_row)
            all_probs.append(jnp.exp(scores - row_max) * inverse)
        direction = 0.0
        for part in range(2):
            finish(*need_grads[part])
            direction = direction + jnp.dot(
                grad_ref[:, part * width : (part + 1) * width],
                weight_ref[part].reshape(width, LOCAL),
                preferred_element_type=F32,
            )
        direction = direction.astype(BF)
        finish(*need_attn)
        total[...] = jnp.zeros_like(total) if first else total_in[...]
        for n, block in enumerate(blocks):
            start = near_start(block)
            probs = all_probs[n]
            keys = window(key_ref, start)
            queries = stacked_heads(query_ref[n])
            out_dir = stacked_heads(direction[n * TOK : (n + 1) * TOK])
            attn = stacked_heads(attn_ref[n])
            delta = jnp.sum(out_dir.astype(F32) * attn.astype(F32), axis=1, keepdims=True)
            dprobs = contract_columns(out_dir, window(value_ref, start))
            dscores = (probs * (dprobs - delta)).astype(BF)
            dquery = (jnp.dot(dscores, keys, preferred_element_type=F32) * FACTOR).astype(BF)
            for h in range(GROUP):
                columns = slice(h * HEAD, (h + 1) * HEAD)
                result_ref[n, :, columns] = dquery[h * TOK : (h + 1) * TOK]
            target = send_hbm.at[tile_rows(block), 0:LOCAL]
            moved.append(copies.start(result_ref.at[n], target))
            dkeys = contract_rows(dscores, queries)
            dvalues = contract_rows(probs.astype(BF), out_dir)
            near = pl.ds(start, NEAR)
            total[0:PROMPT, 0:HEAD] += dkeys[0:PROMPT]
            total[0:PROMPT, HEAD:] += dvalues[0:PROMPT]
            total[near, 0:HEAD] += dkeys[PROMPT:]
            total[near, HEAD:] += dvalues[PROMPT:]
        if last:
            cast_ref[:, 0:HEAD] = (total[:, 0:HEAD] * FACTOR).astype(BF)
            cast_ref[:, HEAD:] = total[:, HEAD:].astype(BF)
            moved.append(copies.start(cast_ref, send_hbm.at[:, LOCAL:]))
        finish(*moved)

    return step_kernel


def attention_step(
    ids, core_arg, seg_row, state, weight, pieces, carried, last=False, keep=False
):
    count, first = len(pieces) // 2, carried is None
    width = pieces[0].shape[1]
    operands = [ids, core_arg, seg_row, *state, weight, *pieces]
    outs = [((PACK, LOCAL + 2 * HEAD), BF)]
    in_vmem, out_vmem, aliases, scratch = [2], (1, 2), {}, []
    if not first:
        operands += carried
        in_vmem.append(len(operands) - 2)
        aliases = {len(operands) - 1: 0}
    if last:
        in_vmem += [6, 7, 8]
        scratch.append(pltpu.VMEM((PACK, 2 * HEAD), F32))
    else:
        outs.append(((PACK, 2 * HEAD), F32))
        if not first:
            aliases[len(operands) - 2] = 1
        held = (2, BLOCKS, HEAD, LOCAL)
        if keep:
            outs.append((held, BF))
        else:
            scratch.append(pltpu.VMEM(held, BF))
    scratch += [
        pltpu.VMEM((count * TOK, 2 * width), BF),
        pltpu.VMEM((PACK, HEAD), BF),
        pltpu.VMEM((PACK, HEAD), BF),
        pltpu.VMEM((count, TOK, LOCAL), BF),
        pltpu.VMEM((count, TOK, LOCAL), BF),
        pltpu.VMEM((count, TOK, 2 * GROUP), F32),
        pltpu.VMEM((count, TOK, LOCAL), BF),
        pltpu.VMEM((PACK, 2 * HEAD), BF),
        pltpu.SemaphoreType.DMA((32,)),
    ]
    return call(
        make_step_kernel(count, first, last),
        2,
        operands,
        outs,
        scratch,
        in_vmem=in_vmem,
        out_vmem=out_vmem,
        aliases=aliases,
        flops=count * 1200000000,
        bytes_accessed=12000000,
    )


def start_chunk(copies, pieces, stage, chunk, place):
    width = stage.shape[2]
    columns = pl.ds(pl.multiple_of(place * width, width), width)
    return [
        copies.start(piece.at[:, columns], stage.at[chunk, n * TOK : (n + 1) * TOK, :])
        for n, piece in enumerate(pieces)
    ]


def start_turned(copies, offsets, turned_hbm, turned_ref):
    return [
        copies.start(
            turned_hbm.at[:, k * TOK : (k + 1) * TOK], turned_ref.at[:, n * TOK : (n + 1) * TOK]
        )
        for n, k in enumerate(offsets)
    ]


def make_weight_kernel(offsets, has_early):
    many = len(offsets)

    def weight_kernel(turned_hbm, *refs):
        pieces, refs = refs[:many], refs[many:]
        if has_early:
            early_hbm, out_hbm, turned_ref, stage, out_ref, early_ref, sems = refs
        else:
            out_hbm, turned_ref, stage, out_ref, sems = refs
        copies, moved = Copies(sems), []
        turned = start_turned(copies, offsets, turned_hbm, turned_ref)
        arriving = []
        for c in range(4):
            arriving.append(start_chunk(copies, pieces, stage, c, c))
            if has_early:
                arriving[c].append(copies.start(early_hbm.at[c], early_ref.at[c]))
        finish(*turned)
        for c in range(4):
            finish(*arriving[c])
            sums = jnp.dot(turned_ref[...], stage[c], preferred_element_type=F32)
            if has_early:
                sums = (sums + early_ref[c].astype(F32)).astype(BF)
                for n in range(4):
                    out_ref[4 * c + n] = sums[:, n * HEAD : (n + 1) * HEAD]
                part = pl.ds(4 * c, 4)
            else:
                out_ref[c] = sums.astype(BF)
                part = c
            moved.append(copies.start(out_ref.at[part], out_hbm.at[part]))
        finish(*moved)

    return weight_kernel


def weight_terms(offsets, turned, pieces, early=None):
    width = pieces[0].shape[1] // 4
    operands = [turned, *pieces]
    out = (4, LOCAL, width) if early is None else (BLOCKS, LOCAL, HEAD)
    scratch = [
        pltpu.VMEM((LOCAL, len(offsets) * TOK), BF),
        pltpu.VMEM((4, len(offsets) * TOK, width), BF),
        pltpu.VMEM(out, BF),
    ]
    if early is not None:
        operands.append(early)
        scratch.append(pltpu.VMEM(early.shape, BF))
    return call(
        make_weight_kernel(offsets, early is not None),
        0,
        operands,
        [(out, BF)],
        scratch + [pltpu.SemaphoreType.DMA((48,))],
        in_vmem=[1 + n for n, k in enumerate(offsets) if k == 4],
        flops=len(offsets) * 270000000,
        bytes_accessed=6 << 20,
    )[0]


def make_mine_kernel(offsets):
    many = len(offsets)

    def mine_kernel(place_ref, turned_hbm, early_hbm, arrived_hbm, *refs):
        pieces, out_refs, refs = refs[:many], refs[many : many + 8], refs[many + 8 :]
        turned_ref, stage, early_ref, arrived_ref, half_x, half_y, sems = refs
        copies, moved, arriving = Copies(sems), [], []
        y, x = place_ref[0], place_ref[1]
        turned = start_turned(copies, offsets, turned_hbm, turned_ref)
        for ky in range(4):
            to_y = lax.rem(y + ky, 4)
            arriving.append(start_chunk(copies, pieces, stage, ky, to_y))
            arriving[ky].append(copies.start(early_hbm.at[to_y], early_ref.at[ky]))
            arriving[ky].append(
                copies.start(arrived_hbm.at[pl.ds(to_y * 4, 4)], arrived_ref.at[ky])
            )
        finish(*turned)
        for ky in range(4):
            to_y = lax.rem(y + ky, 4)
            finish(*arriving[ky])
            sums = jnp.dot(turned_ref[...], stage[ky], preferred_element_type=F32)
            sums = sums + early_ref[ky].astype(F32)
            for to_x in range(4):
                both = sums[:, to_x * HEAD : (to_x + 1) * HEAD]
                both = (both + arrived_ref[ky, to_x].astype(F32)).astype(BF)
                half_x[lax.rem(to_x + 4 - x, 4), to_y] = both[0:X_ROWS]
                half_y[ky, to_x] = both[X_ROWS:]
            if ky:
                moved.append(copies.start(half_y.at[ky], out_refs[4 + ky]))
            else:
                out_refs[4][...] = half_y[0]
        for kx in range(1, 4):
            moved.append(copies.start(half_x.at[kx], out_refs[kx]))
        out_refs[0][...] = half_x[0]
        finish(*moved)

    return mine_kernel


def make_middle_kernel(axis):
    def middle_kernel(place_ref, *refs):
        arrived, outs = refs[0:4], refs[4:8]
        for k in range(4):
            at = lax.rem(place_ref[axis] + k, 4)
            outs[k][...] = sum(ref[at].astype(F32) for ref in arrived).astype(outs[k].dtype)

    return middle_kernel


def make_final_kernel(scale):
    def final_kernel(*refs):
        out_ref = refs[8]
        parts = [sum(ref[...].astype(F32) for ref in refs[4 * n : 4 * n + 4]) for n in range(2)]
        out_ref[...] = jnp.concatenate(parts, axis=0).T * scale

    return final_kernel


def call(
    kernel,
    scalars,
    operands,
    outs,
    scratch=(),
    in_vmem=(),
    out_vmem=(),
    aliases=None,
    flops=0,
    bytes_accessed=0,
):
    in_specs, placed = [], []
    for n, value in enumerate(operands):
        if n < scalars:
            in_specs.append(SMEM)
        elif n in in_vmem:
            in_specs.append(VMEM)
        else:
            in_specs.append(HBM)
            value = pltpu.with_memory_space_constraint(value, pltpu.HBM)
        placed.append(value)
    return pl.pallas_call(
        kernel,
        out_shape=[
            jax.ShapeDtypeStruct(dims, dtype) if n in out_vmem else pltpu.HBM(dims, dtype)
            for n, (dims, dtype) in enumerate(outs)
        ],
        in_specs=in_specs,
        out_specs=[VMEM if n in out_vmem else HBM for n in range(len(outs))],
        scratch_shapes=list(scratch),
        input_output_aliases=aliases or {},
        compiler_params=params(),
        cost_estimate=cost(flops, bytes_accessed),
    )(*placed)


def call_vmem(kernel, scalars, operands, outs, bytes_accessed):
    return pl.pallas_call(
        kernel,
        out_shape=[jax.ShapeDtypeStruct(dims, dtype) for dims, dtype in outs],
        in_specs=[SMEM] * scalars + [VMEM] * (len(operands) - scalars),
        out_specs=[VMEM] * len(outs),
        compiler_params=params(),
        cost_estimate=cost(0, bytes_accessed),
    )(*operands)


def exchange(value):
    return lax.all_to_all(value, "head", split_axis=0, concat_axis=0, tiled=True)


def along_ring(value, shift):
    return lax.ppermute(value, "head", [(i, (i + shift) % RING) for i in range(RING)])


def along_dp(value, dy, dx, dcore):
    pairs = []
    for y in range(4):
        for x in range(4):
            for core in range(2):
                to = (((y + dy) % 4) * 4 + (x + dx) % 4) * 2 + (core + dcore) % 2
                pairs.append(((y * 4 + x) * 2 + core, to))
    return lax.ppermute(value, "dp", pairs)


def shards(query_states, key_states, value_columns, seg_ids, out_grad, out_weight):
    width = out_grad.shape[2]
    half = width // 2
    kv_width = KEY_VALUE_HEADS * HEAD
    joint = (RING, TOK, LOCAL + 2 * HEAD)
    me = lax.axis_index("head").astype(jnp.int32)
    dp = lax.axis_index("dp").astype(jnp.int32)
    me_arg, core_arg = me[None], (dp % 2)[None]
    place = jnp.stack([dp // 8, (dp // 2) % 4])
    weight_blocks = out_weight.reshape(BLOCKS, 2, HEAD, LOCAL)

    (packed,) = call(
        pack_kernel,
        0,
        [query_states[0], key_states[0], value_columns[0]],
        [(joint, BF)],
        [
            pltpu.VMEM((TOK, width), BF),
            pltpu.VMEM((TOK, kv_width), BF),
            pltpu.VMEM((TOK, kv_width), BF),
            pltpu.SemaphoreType.DMA((2 + 4 * RING,)),
        ],
        bytes_accessed=3 << 20,
    )
    other0, mine0 = call(
        split_kernel,
        1,
        [core_arg, out_grad[0]],
        [((TOK, half), BF), ((TOK, half), BF)],
        [pltpu.VMEM((TOK, width), BF), pltpu.SemaphoreType.DMA((4 + 2 * BLOCKS,))],
        bytes_accessed=2 << 20,
    )
    up, down = [[other0], [mine0]], [[other0], [mine0]]

    def ring_step(part, *before):
        moved = along_ring(up[part][-1], 1), along_ring(down[part][-1], -1)
        moved, before = lax.optimization_barrier((moved, before))
        up[part].append(moved[0])
        down[part].append(moved[1])
        return before

    pack = exchange(packed).reshape(PACK, LOCAL + 2 * HEAD)
    (pack,) = ring_step(0, pack)
    attn, turned, stat = call(
        forward_kernel,
        1,
        [me_arg, seg_ids, pack],
        [((PACK, LOCAL), BF), ((LOCAL, PACK), BF), ((PACK, 2 * GROUP), F32)],
        [
            pltpu.VMEM((PACK, LOCAL), BF),
            pltpu.VMEM((PACK, HEAD), BF),
            pltpu.VMEM((PACK, HEAD), BF),
            pltpu.VMEM((PACK, LOCAL), BF),
            pltpu.VMEM((LOCAL, PACK), BF),
            pltpu.VMEM((PACK, 2 * GROUP), F32),
            pltpu.SemaphoreType.DMA((6,)),
        ],
        in_vmem=(1,),
        flops=1400000000,
        bytes_accessed=5 << 20,
    )
    (attn,) = ring_step(1, attn)

    def by_offset(part, offsets, far=None):
        found = {0: up[part][0], 4: far}
        for s in range(1, len(up[part])):
            found[s], found[RING - s] = down[part][s], up[part][s]
        return [found[k] for k in offsets]

    near, far_off = (0, 1, 7), (2, 3, 4, 5, 6)
    close, distant = (0, 1, 2, 6, 7), (3, 4, 5)
    other_early = weight_terms(near, turned, by_offset(0, near))
    (other_early,) = ring_step(0, other_early)
    state = (pack, attn, stat)

    def both_ways(s):
        ids = [(me + RING - s) % RING, (me + s) % RING]
        return ids, [up[0][s], up[1][s], down[0][s], down[1][s]]

    def step(ids, pieces, carried, keep=False):
        send, total, *weight = attention_step(
            jnp.stack(ids), core_arg, seg_ids, state, weight_blocks, pieces, carried, keep=keep
        )
        return [total, send] + weight

    ids, pieces = both_ways(1)
    total, send = step([me] + ids, [other0, mine0] + pieces, None)
    (total,) = ring_step(1, total)
    mine_early = weight_terms(close, turned, by_offset(1, close))
    (mine_early,) = ring_step(0, mine_early)
    total, send = step(*both_ways(2), [total, send])
    other_far = along_ring(up[0][3], 1)
    (total,) = ring_step(1, total)
    mine_far = along_ring(down[1][3], -1)
    total, send, weight = step(*both_ways(3), [total, send], keep=True)
    other_far, total = lax.optimization_barrier((other_far, total))

    other = weight_terms(far_off, turned, by_offset(0, far_off, other_far), other_early)
    from_core = along_dp(other, 0, 0, 1)
    mine_far, total, other = lax.optimization_barrier((mine_far, total, other))
    (send,) = attention_step(
        ((me + 4) % RING)[None],
        core_arg,
        seg_ids,
        state,
        weight,
        [other_far, mine_far],
        [total, send],
        last=True,
    )
    turned, send = lax.optimization_barrier((turned, send))
    chunks = (4, len(distant) * TOK, half // 4)
    halves = call(
        make_mine_kernel(distant),
        1,
        [place, turned, mine_early, from_core, *by_offset(1, distant, mine_far)],
        [((4, rows, HEAD), BF) for rows in SHARES for _ in range(4)],
        [
            pltpu.VMEM((LOCAL, len(distant) * TOK), BF),
            pltpu.VMEM(chunks, BF),
            pltpu.VMEM(mine_early.shape, BF),
            pltpu.VMEM((4, 4, LOCAL, HEAD), BF),
            pltpu.VMEM((4, 4, SHARES[0], HEAD), BF),
            pltpu.VMEM((4, 4, SHARES[1], HEAD), BF),
            pltpu.SemaphoreType.DMA((48,)),
        ],
        in_vmem=[4 + n for n, k in enumerate(distant) if k == 4],
        out_vmem=(0, 4),
        flops=800000000,
        bytes_accessed=9 << 20,
    )
    received = exchange(send.reshape(joint))
    shares = []
    for axis in range(2):
        own_half = halves[4 * axis : 4 * axis + 4]
        steps = [(0, k, 0) if axis == 0 else (k, 0, 0) for k in range(4)]
        arrived = [own_half[0]] + [along_dp(own_half[k], *steps[k]) for k in range(1, 4)]
        middle = call_vmem(
            make_middle_kernel(axis),
            1,
            [place, *arrived],
            [((SHARES[axis], HEAD), F32)] + [((SHARES[axis], HEAD), BF)] * 3,
            2 << 20,
        )
        steps = [(k, 0, 0) if axis == 0 else (0, k, 0) for k in range(4)]
        shares += [middle[0]] + [along_dp(middle[k], *steps[k]) for k in range(1, 4)]
    query_gradient, key_gradient, value_gradient = call(
        spread_kernel,
        0,
        [received],
        [((TOK, width), BF), ((TOK, kv_width), BF), ((TOK, kv_width), BF)],
        [pltpu.SemaphoreType.DMA((3 * RING,))],
        in_vmem=(0,),
        bytes_accessed=3 << 20,
    )
    shares[7], query_gradient = lax.optimization_barrier((shares[7], query_gradient))
    weight_grad = pl.pallas_call(
        make_final_kernel(1.0 / math.sqrt(lax.axis_size("dp") * PACK)),
        out_shape=jax.ShapeDtypeStruct((HEAD, LOCAL), F32),
        compiler_params=params(),
        cost_estimate=cost(0, 1 << 20),
    )(*shares)
    return (query_gradient[None], key_gradient[None], value_gradient[None], weight_grad)


def solution(mesh):
    in_specs = (
        P("dp", "head", None),
        P("dp", "head", None),
        P("dp", "head", None),
        P("dp", None),
        P("dp", "head", None),
        P(None, "head"),
    )
    out_specs = (
        P("dp", "head", None),
        P("dp", "head", None),
        P("dp", "head", None),
        P("dp", "head"),
    )
    return jax.shard_map(shards, mesh=mesh, in_specs=in_specs, out_specs=out_specs, check_vma=False)
```
